32 devices in a mesh: gz: 4 (over x, core), xy: 8 (over z, y).
Axes of the slice: x: 2, y: 2, z: 4, core: 2. Of those that a mesh axis runs over, the one named last changes fastest.
Arguments:
- features: float32 [64, 16, 28, 256], P('gz', 'xy'), may hold values from -6 to 6
- block_mask: int32 [32, 8, 14], P('gz', 'xy'), may hold values 0 or 1
- near_kernel_weight: float32 [27, 256, 256], P(None, None, 'xy'), may hold values from -0.078125 to 0.078125
- far_kernel_weight: float32 [27, 256, 256], P(None, None, 'xy'), may hold values from -0.078125 to 0.078125
Outputs:
- section_out: float32 [64, 16, 28, 256], P('gz', 'xy')
The draws below stay inside these ranges and needn't reach their ends.
All inputs are finite; a program needn't handle non-finite values. No bound on the sum of `block_mask` on one device may be relied on, other than what follows from the above.
Results may differ from the reference program's by a relative error of at most 0.00005.
Values sent between devices are 32-bit elements; how exact they have to be, the bound alone decides.
A program may use at most 128 MiB of HBM per device.

```python
import jax
import jax.numpy as jnp
from jax import lax

C = 256
B = 2
NEAR_DILATION = 16
FAR_DILATION = 32
NY = 28
NZ = 64
NX = 16


def set_ends(values, own_key, least, top_value):
    longest = values.shape.index(max(values.shape))
    spots = []
    for shift in (0, 1):
        where = [jax.random.randint(jax.random.fold_in(own_key, axis), (), 0, length) for axis, length in enumerate(values.shape)]
        where[longest] = (where[longest] + shift) % values.shape[longest]
        spots.append(tuple(where))
    return values.at[spots[0]].set(least).at[spots[1]].set(top_value)


def shard_levels(stream_key, extent, split, least, top_value):
    def one(dim, blocks):
        heights = jax.random.uniform(jax.random.fold_in(jax.random.fold_in(stream_key, 6), dim), (blocks,), jnp.float32, least / len(split), top_value / len(split))
        return jnp.repeat(jnp.exp(heights), extent[dim] // blocks).reshape((-1,) + (1,) * (len(extent) - dim - 1))

    loudness = one(*split[0])
    for cut in split[1:]:
        loudness = loudness * one(*cut)
    return loudness


def noise(rng, extent, width, most, cuts=(), dtype=jnp.bfloat16):
    entries = width * jax.random.normal(rng, extent, jnp.float32)
    if cuts:
        entries = entries * shard_levels(rng, extent, cuts, -0.22, 0.18)
    return jnp.clip(entries, -most, most).astype(dtype)


def setup_inputs(seed: int = 0) -> dict:
    keys = jax.random.split(jax.random.key(seed), 5)
    return {
        "features": noise(keys[0], (NZ, NX, NY, C), 1.0, 6.0, ((0, 4), (1, 8)), jnp.float32),
        "block_mask": set_ends((jax.random.randint(keys[1], (NZ // B, NX // B, NY // B), 0, 5) < 3).astype(jnp.int32), jax.random.fold_in(keys[1], 1), 0, 1),
        "near_kernel_weight": noise(keys[2], (27, C, C), (27 * C) ** -0.5, 0.078125, ((2, 8),), jnp.float32),
        "far_kernel_weight": noise(keys[3], (27, C, C), (27 * C) ** -0.5, 0.078125, ((2, 8),), jnp.float32),
    }


def dilated_result(field, weight, dilation):
    channels = weight.shape[1]
    kernel = weight.reshape(3, 3, 3, channels, weight.shape[2])
    result = lax.conv_general_dilated(
        field[None], kernel, (1, 1, 1), [(dilation, dilation)] * 3,
        rhs_dilation=(dilation, dilation, dilation),
        dimension_numbers=("NDHWC", "DHWIO", "NDHWC"),
        precision=lax.Precision.HIGHEST)
    return result[0]


def reference(features, block_mask, near_kernel_weight, far_kernel_weight):
    active_blocks = jnp.repeat(jnp.repeat(jnp.repeat(block_mask, B, 0), B, 1), B, 2)
    active_blocks = active_blocks.astype(jnp.float32)[..., None]
    masked_input = active_blocks * features
    hidden_state = active_blocks * jnp.maximum(dilated_result(masked_input, near_kernel_weight, NEAR_DILATION), 0.0)
    return active_blocks * (masked_input + dilated_result(hidden_state, far_kernel_weight, FAR_DILATION))
```

```python
import jax
import jax.numpy as jnp
from jax import lax
from jax.sharding import PartitionSpec as P

B = 2
NEAR_DILATION = 16
FAR_DILATION = 32


def offsets(dilation, extent):
    return (-1, 0, 1) if dilation < extent else (0,)


def from_behind(block, axis, distance):
    if distance == 0:
        return block
    devices = range(lax.axis_size(axis))
    route = [(i - distance, i) for i in devices if i - distance in devices]
    return lax.ppermute(block, axis, route)


def reach(field, dilation):
    slab_z, slab_x, span_y, _ = field.shape
    return (
        offsets(dilation, slab_z * lax.axis_size("gz")),
        offsets(dilation, slab_x * lax.axis_size("xy")),
        offsets(dilation, span_y),
    )


def gathered(weight, taps):
    cube = weight.reshape((3, 3, 3) + weight.shape[1:])
    for dim, tap in enumerate(taps):
        cube = cube if len(tap) == 3 else lax.slice_in_dim(cube, 1, 2, axis=dim)
    flat = cube.reshape((-1,) + weight.shape[1:])
    return lax.all_gather(flat, "xy", axis=2, tiled=True)


def dilated_result(field, weight, taps, dilation):
    slab_z, slab_x, span_y, channels = field.shape
    windows = []
    for a in taps[0]:
        over_z = from_behind(field, "gz", -a * dilation // slab_z)
        for b in taps[1]:
            over_x = from_behind(over_z, "xy", -b * dilation // slab_x)
            for c in taps[2]:
                if c == 0:
                    windows.append(over_x)
                elif c < 0:
                    part = over_x[:, :, : span_y - dilation]
                    windows.append(jnp.pad(part, ((0, 0), (0, 0), (dilation, 0), (0, 0))))
                else:
                    part = over_x[:, :, dilation:]
                    windows.append(jnp.pad(part, ((0, 0), (0, 0), (0, dilation), (0, 0))))
    columns = jnp.concatenate(windows, 3).reshape(slab_z * slab_x * span_y, -1)
    summed = jnp.dot(
        columns,
        weight.reshape(-1, weight.shape[2]),
        precision=lax.Precision.HIGH,
        preferred_element_type=jnp.float32,
    )
    return summed.reshape(slab_z, slab_x, span_y, weight.shape[2])


def local(features, block_mask, near_kernel_weight, far_kernel_weight):
    near_taps = reach(features, NEAR_DILATION)
    far_taps = reach(features, FAR_DILATION)
    active = jnp.repeat(jnp.repeat(jnp.repeat(block_mask, B, 0), B, 1), B, 2)
    active = active.astype(jnp.float32)[..., None]
    near_weight = gathered(near_kernel_weight, near_taps)
    far_weight = gathered(far_kernel_weight, far_taps)
    masked = active * features
    hidden = active * jnp.maximum(
        dilated_result(masked, near_weight, near_taps, NEAR_DILATION), 0.0
    )
    return active * (masked + dilated_result(hidden, far_weight, far_taps, FAR_DILATION))


def solution(mesh):
    in_specs = (
        P("gz", "xy", None, None),
        P("gz", "xy", None),
        P(None, None, "xy"),
        P(None, None, "xy"),
    )
    out_specs = P("gz", "xy", None, None)
    return jax.shard_map(local, mesh=mesh, in_specs=in_specs, out_specs=out_specs, check_vma=False)
```

```python
import functools

import jax
import jax.numpy as jnp
from jax import lax
from jax.experimental import pallas as pl
from jax.experimental.pallas import tpu as pltpu
from jax.sharding import PartitionSpec as P

B = 2
NEAR_DILATION = 16
FAR_DILATION = 32
MESH = pl.DeviceIdType.MESH
GROUP = 2


def offsets(dilation, extent):
    return (-1, 0, 1) if dilation < extent else (0,)


def from_behind(block, axis, distance):
    if distance == 0:
        return block
    devices = range(lax.axis_size(axis))
    route = [(i - distance, i) for i in devices if i - distance in devices]
    return lax.ppermute(block, axis, route)


def reach(field, dilation):
    slab_z, slab_x, span_y, _ = field.shape
    return (
        offsets(dilation, slab_z * lax.axis_size("gz")),
        offsets(dilation, slab_x * lax.axis_size("xy")),
        offsets(dilation, span_y),
    )


def gathered(weight, taps):
    cube = weight.reshape((3, 3, 3) + weight.shape[1:])
    for dim, tap in enumerate(taps):
        cube = cube if len(tap) == 3 else lax.slice_in_dim(cube, 1, 2, axis=dim)
    flat = cube.reshape((-1,) + weight.shape[1:])
    return lax.all_gather(flat, "xy", axis=2, tiled=True)


def dilated_result(field, weight, taps, dilation):
    slab_z, slab_x, span_y, channels = field.shape
    windows = []
    for a in taps[0]:
        over_z = from_behind(field, "gz", -a * dilation // slab_z)
        for b in taps[1]:
            over_x = from_behind(over_z, "xy", -b * dilation // slab_x)
            for c in taps[2]:
                if c == 0:
                    windows.append(over_x)
                elif c < 0:
                    part = over_x[:, :, : span_y - dilation]
                    windows.append(jnp.pad(part, ((0, 0), (0, 0), (dilation, 0), (0, 0))))
                else:
                    part = over_x[:, :, dilation:]
                    windows.append(jnp.pad(part, ((0, 0), (0, 0), (0, dilation), (0, 0))))
    columns = jnp.concatenate(windows, 3).reshape(slab_z * slab_x * span_y, -1)
    summed = jnp.dot(
        columns,
        weight.reshape(-1, weight.shape[2]),
        precision=lax.Precision.HIGH,
        preferred_element_type=jnp.float32,
    )
    return summed.reshape(slab_z, slab_x, span_y, weight.shape[2])


def general(features, block_mask, near_kernel_weight, far_kernel_weight):
    near_taps = reach(features, NEAR_DILATION)
    far_taps = reach(features, FAR_DILATION)
    active = jnp.repeat(jnp.repeat(jnp.repeat(block_mask, B, 0), B, 1), B, 2)
    active = active.astype(jnp.float32)[..., None]
    near_weight = gathered(near_kernel_weight, near_taps)
    far_weight = gathered(far_kernel_weight, far_taps)
    masked = active * features
    hidden = active * jnp.maximum(
        dilated_result(masked, near_weight, near_taps, NEAR_DILATION), 0.0
    )
    return active * (masked + dilated_result(hidden, far_weight, far_taps, FAR_DILATION))


def section_kernel(
    n, deep, span_y, near_step, far_step,
    feat, mask, near, far, out,
    wall, stage, xs, ms, mf, xc, xl, xh, acc, hc,
    up_send, down_send, pair_send, core_send, line_recv, pair_recv, core_recv,
    x_send, x_recv, m_send, m_recv, r_send, r_recv, load_sem, own_sem,
):
    taps, wide, channels = wall.shape
    part = near.shape[1]
    half = part // 2
    positions = wide // part
    line = positions // 2
    groups = taps // GROUP
    rows = xs.shape[1]
    plane = rows // deep
    skip = plane * NEAR_DILATION // span_y
    edge = plane - skip
    side = deep * edge
    near_taps = 9

    g = lax.axis_index("gz")
    s = lax.axis_index("xy")
    pos, col = s // 2, s % 2
    core = g % 2
    twin = g + 1 - 2 * core
    mate = s + 1 - 2 * col

    home = pl.ds(pl.multiple_of(s * part, part), part)
    loads = []
    for a in range(3):
        loads.append((near.at[pl.ds(9 * a + 3, 3)], wall.at[pl.ds(3 * a, 3), home, :]))
    for a in range(3):
        loads.append((far.at[pl.ds(9 * a + 4, 1)], wall.at[pl.ds(near_taps + a, 1), home, :]))
    loads.append((feat.at[g], xs.at[g]))
    loads = [pltpu.make_async_copy(a, b, load_sem.at[i]) for i, (a, b) in enumerate(loads)]
    for load in loads:
        load.start()

    barrier = pltpu.get_barrier_semaphore()
    for i in range(1, n):
        pl.semaphore_signal(barrier, inc=1, device_id={"gz": (g + i) % n}, device_id_type=MESH)
    pl.semaphore_signal(barrier, inc=1, device_id={"xy": mate}, device_id_type=MESH)

    @pl.when(pos > 0)
    def _():
        pl.semaphore_signal(barrier, inc=1, device_id={"xy": s - 2}, device_id_type=MESH)

    @pl.when(pos < line - 1)
    def _():
        pl.semaphore_signal(barrier, inc=1, device_id={"xy": s + 2}, device_id_type=MESH)

    ms[g] = mask[g]
    for load in loads:
        load.wait()

    @pl.when((pos > 0) & (pos < line - 1))
    def _():
        pl.semaphore_wait(barrier, n + 2)

    @pl.when((pos == 0) | (pos == line - 1))
    def _():
        pl.semaphore_wait(barrier, n + 1)

    def piece(p, q, h, grp):
        start = pl.multiple_of((2 * p + q) * part + h * half, half)
        return wall.at[pl.ds(GROUP * grp, GROUP), pl.ds(start, half), :]

    def up(p, grp):
        ref = piece(p, col, core, grp)
        return pltpu.make_async_remote_copy(
            ref, ref, up_send.at[p, grp], line_recv.at[p, grp], device_id={"xy": s + 2}, device_id_type=MESH)

    def down(p, grp):
        ref = piece(p, col, core, grp)
        return pltpu.make_async_remote_copy(
            ref, ref, down_send.at[p, grp], line_recv.at[p, grp], device_id={"xy": s - 2}, device_id_type=MESH)

    def across(p, q, grp):
        ref = piece(p, q, core, grp)
        return pltpu.make_async_remote_copy(
            ref, ref, pair_send.at[p, grp], pair_recv.at[p, grp], device_id={"xy": mate}, device_id_type=MESH)

    def to_twin(p, q, h, grp):
        ref = piece(p, q, h, grp)
        where = 2 * p + q
        return pltpu.make_async_remote_copy(
            ref, ref, core_send.at[where, grp], core_recv.at[where, grp], device_id={"gz": twin}, device_id_type=MESH)

    def both(t, act):
        @pl.when(pos - t >= 0)
        def _():
            act(pos - t)

        if t > 0:
            @pl.when(pos + t < line)
            def _():
                act(pos + t)

    def line_stage(t, grp):
        @pl.when(pos - t >= 0)
        def _():
            if t > 0:
                up(pos - t, grp).wait_recv()

            @pl.when(pos + 1 < line)
            def _():
                up(pos - t, grp).start()

            across(pos - t, col, grp).start()
            if t > 0:
                to_twin(pos - t, col, core, grp).start()

        @pl.when(pos + t < line)
        def _():
            if t > 0:
                down(pos + t, grp).wait_recv()

            @pl.when(pos >= 1)
            def _():
                down(pos + t, grp).start()

            if t > 0:
                across(pos + t, col, grp).start()
                to_twin(pos + t, col, core, grp).start()

    def pair_stage(t, grp):
        def act(p):
            across(p, 1 - col, grp).wait_recv()
            to_twin(p, 1 - col, core, grp).start()

        both(t, act)

    def core_stage(t, grp):
        def act(p):
            if t > 0:
                to_twin(p, col, 1 - core, grp).wait_recv()
            to_twin(p, 1 - col, 1 - core, grp).wait_recv()

        both(t, act)

    def finish(t, grp):
        @pl.when(pos - t >= 0)
        def _():
            @pl.when(pos + 1 < line)
            def _():
                up(pos - t, grp).wait_send()

            across(pos - t, col, grp).wait_send()
            to_twin(pos - t, 1 - col, core, grp).wait_send()
            if t > 0:
                to_twin(pos - t, col, core, grp).wait_send()

        @pl.when(pos + t < line)
        def _():
            @pl.when(pos >= 1)
            def _():
                down(pos + t, grp).wait_send()

            if t > 0:
                across(pos + t, col, grp).wait_send()
                to_twin(pos + t, 1 - col, core, grp).wait_send()
                to_twin(pos + t, col, core, grp).wait_send()

    def exchange(src, dst, send, recv, d):
        return pltpu.make_async_remote_copy(
            src.at[d], dst.at[g], send.at[d], recv.at[g], device_id={"gz": d}, device_id_type=MESH)

    def arrival(dst, send, recv, d):
        return pltpu.make_async_remote_copy(
            dst.at[d], dst.at[d], send.at[d], recv.at[d], device_id={"gz": d}, device_id_type=MESH)

    def split(value, ref, start, count):
        high = value.astype(jnp.bfloat16)
        low = (value - high.astype(jnp.float32)).astype(jnp.bfloat16)
        at = pl.ds(start, count)
        ref[at, 0:channels] = high
        ref[at, channels : 2 * channels] = low
        ref[at, 2 * channels :] = high

    def tap_weight(tap):
        value = wall[tap]
        high = value.astype(jnp.bfloat16)
        low = (value - high.astype(jnp.float32)).astype(jnp.bfloat16)
        return jnp.concatenate([high, high, low], axis=1)

    def product(lhs, weight):
        return lax.dot_general(lhs, weight, (((1,), (1,)), ((), ())), preferred_element_type=jnp.float32)

    def near_tap(tap):
        a, c = tap // 3 - 1, tap % 3 - 1
        first, last = max(0, a * near_step), min(n, n + a * near_step)
        if first >= last:
            return
        weight = tap_weight(tap)
        to = first - a * near_step
        if c == 0:
            acc[to * rows : (to + last - first) * rows] += product(xc[first * rows : last * rows], weight)
        else:
            source, offset = (xl, skip) if c < 0 else (xh, 0)
            result = product(source[first * side : last * side], weight)
            for i in range((last - first) * deep):
                base = to * rows + i * plane + offset
                acc[base : base + edge] += result[i * edge : (i + 1) * edge]

    def far_tap(tap):
        a = tap - near_taps - 1
        first, last = max(0, a * far_step), min(n, n + a * far_step)
        if first >= last:
            return
        to = first - a * far_step
        acc[to * rows : (to + last - first) * rows] += product(hc[first * rows : last * rows], tap_weight(tap))

    def turn():
        for i in range(n):
            at = slice(i * rows, (i + 1) * rows)
            keep = mf[at]
            value = jnp.maximum(acc[at], 0.0) * jnp.concatenate([keep] * (channels // 128), axis=1)
            split(value, hc, i * rows, rows)
            acc[at] = xs[i]

    def take_features():
        for i in range(1, n):
            d = (g + i) % n
            arrival(xs, x_send, x_recv, d).wait_recv()
            arrival(ms, m_send, m_recv, d).wait_recv()
        flags = [ms[i] for i in range(n)]
        flags.append(jnp.zeros((128 - n * 8, 128), jnp.float32))
        flags = jnp.transpose(jnp.concatenate(flags, axis=0))
        for i in range(n):
            value = xs[i]
            split(value, xc, i * rows, rows)
            planes = [value[z * plane : (z + 1) * plane] for z in range(deep)]
            split(jnp.concatenate([one[:edge] for one in planes], axis=0), xl, i * side, side)
            split(jnp.concatenate([one[skip:] for one in planes], axis=0), xh, i * side, side)
            for z in range(deep):
                column = flags[:plane, i * 8 + z : i * 8 + z + 1]
                mf[i * rows + z * plane : i * rows + (z + 1) * plane, :] = jnp.broadcast_to(column, (plane, 128))
        acc[...] = jnp.zeros_like(acc)

    def compute(grp):
        if grp == 0:
            take_features()
        for tap in range(grp * GROUP, (grp + 1) * GROUP):
            if tap == near_taps:
                turn()
            if tap < near_taps:
                near_tap(tap)
            else:
                far_tap(tap)

    for tau in range(groups + line + 1):
        for t in range(line):
            if 0 <= tau - t < groups:
                line_stage(t, tau - t)
        for t in range(line):
            if 0 <= tau - 1 - t < groups:
                pair_stage(t, tau - 1 - t)
        if tau == 0:
            for i in (2, 1, 3) if n == 4 else range(1, n):
                d = (g + i) % n
                exchange(feat, xs, x_send, x_recv, d).start()
                exchange(mask, ms, m_send, m_recv, d).start()
        grp = tau - line - 1
        if 0 <= grp < groups:
            for t in range(line):
                core_stage(t, grp)
            compute(grp)

    for i in (2, 1, 3) if n == 4 else range(1, n):
        d = (g + i) % n
        at = pl.ds(pl.multiple_of(d * rows, rows), rows)
        exchange(feat, xs, x_send, x_recv, d).wait_send()
        stage[d] = acc[at] * jnp.concatenate([mf[at]] * (channels // 128), axis=1)
        exchange(stage, out, r_send, r_recv, d).start()
    at = pl.ds(pl.multiple_of(g * rows, rows), rows)
    stage[g] = acc[at] * jnp.concatenate([mf[at]] * (channels // 128), axis=1)
    own = pltpu.make_async_copy(stage.at[g], out.at[g], own_sem)
    own.start()
    for grp in range(groups):
        for t in range(line):
            finish(t, grp)
    own.wait()
    for i in range(1, n):
        d = (g + i) % n
        exchange(mask, ms, m_send, m_recv, d).wait_send()
        exchange(stage, out, r_send, r_recv, d).wait_send()
        arrival(out, r_send, r_recv, d).wait_recv()


def fits(features, weight):
    slab_z, slab_x, span_y, channels = features.shape
    n, m = lax.axis_size("gz"), lax.axis_size("xy")
    deep, plane, part = slab_z // n, span_y * slab_x, weight.shape[2]
    return (
        FAR_DILATION >= span_y > NEAR_DILATION
        and NEAR_DILATION >= slab_x * m
        and NEAR_DILATION % slab_z == 0 and FAR_DILATION % slab_z == 0
        and n % 2 == 0 and m % 2 == 0 and m >= 4
        and slab_z % n == 0 and deep <= 8 and n <= 16
        and plane <= 128 and plane % 8 == 0 and NEAR_DILATION * slab_x % 8 == 0
        and deep * plane % 16 == 0 and deep * (span_y - NEAR_DILATION) * slab_x % 16 == 0
        and channels % 128 == 0 and part % 16 == 0 and part * m == channels
    )


def fast(features, block_mask, near_kernel_weight, far_kernel_weight):
    slab_z, slab_x, span_y, channels = features.shape
    n, m = lax.axis_size("gz"), lax.axis_size("xy")
    part = near_kernel_weight.shape[2]
    deep, plane = slab_z // n, span_y * slab_x
    rows, side = deep * plane, deep * (span_y - NEAR_DILATION) * slab_x
    near = jnp.swapaxes(near_kernel_weight, 1, 2)
    far = jnp.swapaxes(far_kernel_weight, 1, 2)
    active = jnp.repeat(jnp.repeat(jnp.repeat(block_mask, B, 0), B, 1), B, 2).astype(jnp.float32)
    active = jnp.swapaxes(active, 1, 2)
    feat = (active[..., None] * jnp.swapaxes(features, 1, 2)).reshape(n, rows, channels)
    mask = jnp.pad(active.reshape(n, deep, plane), ((0, 0), (0, 8 - deep), (0, 128 - plane)))
    taps = 12
    groups, line = taps // GROUP, m // 2
    dma = pltpu.SemaphoreType.DMA
    vmem, hbm = pl.BlockSpec(memory_space=pltpu.VMEM), pl.BlockSpec(memory_space=pl.ANY)
    out = pl.pallas_call(
        functools.partial(section_kernel, n, deep, span_y, NEAR_DILATION // slab_z, FAR_DILATION // slab_z),
        out_shape=jax.ShapeDtypeStruct((n, rows, channels), jnp.float32),
        in_specs=[hbm, vmem, hbm, hbm],
        out_specs=hbm,
        scratch_shapes=[
            pltpu.VMEM((taps, m * part, channels), jnp.float32),
            pltpu.VMEM((n, rows, channels), jnp.float32),
            pltpu.VMEM((n, rows, channels), jnp.float32),
            pltpu.VMEM((n, 8, 128), jnp.float32),
            pltpu.VMEM((n * rows, 128), jnp.float32),
            pltpu.VMEM((n * rows, 3 * channels), jnp.bfloat16),
            pltpu.VMEM((n * side, 3 * channels), jnp.bfloat16),
            pltpu.VMEM((n * side, 3 * channels), jnp.bfloat16),
            pltpu.VMEM((n * rows, channels), jnp.float32),
            pltpu.VMEM((n * rows, 3 * channels), jnp.bfloat16),
            dma((line, groups)), dma((line, groups)), dma((line, groups)), dma((m, groups)),
            dma((line, groups)), dma((line, groups)), dma((m, groups)),
            dma((n,)), dma((n,)), dma((n,)), dma((n,)), dma((n,)), dma((n,)), dma((7,)), dma,
        ],
        compiler_params=pltpu.CompilerParams(
            collective_id=0, has_side_effects=True, vmem_limit_bytes=48 * 1024 * 1024),
        cost_estimate=pl.CostEstimate(flops=3 * 10**9, bytes_accessed=4 * 10**6, transcendentals=0),
    )(feat, mask, near, far)
    return jnp.swapaxes(out.reshape(slab_z, span_y, slab_x, channels), 1, 2)


def local(features, block_mask, near_kernel_weight, far_kernel_weight):
    form = fast if fits(features, near_kernel_weight) else general
    return form(features, block_mask, near_kernel_weight, far_kernel_weight)


def solution(mesh):
    in_specs = (
        P("gz", "xy", None, None),
        P("gz", "xy", None),
        P(None, None, "xy"),
        P(None, None, "xy"),
    )
    out_specs = P("gz", "xy", None, None)
    return jax.shard_map(local, mesh=mesh, in_specs=in_specs, out_specs=out_specs, check_vma=False)
```

```python
import functools

import jax
import jax.numpy as jnp
from jax import lax
from jax.experimental import pallas as pl
from jax.experimental.pallas import tpu as pltpu
from jax.sharding import PartitionSpec as P

B = 2
NEAR_DILATION = 16
FAR_DILATION = 32
MESH = pl.DeviceIdType.MESH


def offsets(dilation, extent):
    return (-1, 0, 1) if dilation < extent else (0,)


def from_behind(block, axis, distance):
    if distance == 0:
        return block
    devices = range(lax.axis_size(axis))
    route = [(i - distance, i) for i in devices if i - distance in devices]
    return lax.ppermute(block, axis, route)


def reach(field, dilation):
    slab_z, slab_x, span_y, _ = field.shape
    return (
        offsets(dilation, slab_z * lax.axis_size("gz")),
        offsets(dilation, slab_x * lax.axis_size("xy")),
        offsets(dilation, span_y),
    )


def gathered(weight, taps):
    cube = weight.reshape((3, 3, 3) + weight.shape[1:])
    for dim, tap in enumerate(taps):
        cube = cube if len(tap) == 3 else lax.slice_in_dim(cube, 1, 2, axis=dim)
    flat = cube.reshape((-1,) + weight.shape[1:])
    return lax.all_gather(flat, "xy", axis=2, tiled=True)


def dilated_result(field, weight, taps, dilation):
    slab_z, slab_x, span_y, channels = field.shape
    windows = []
    for a in taps[0]:
        over_z = from_behind(field, "gz", -a * dilation // slab_z)
        for b in taps[1]:
            over_x = from_behind(over_z, "xy", -b * dilation // slab_x)
            for c in taps[2]:
                if c == 0:
                    windows.append(over_x)
                elif c < 0:
                    part = over_x[:, :, : span_y - dilation]
                    windows.append(jnp.pad(part, ((0, 0), (0, 0), (dilation, 0), (0, 0))))
                else:
                    part = over_x[:, :, dilation:]
                    windows.append(jnp.pad(part, ((0, 0), (0, 0), (0, dilation), (0, 0))))
    columns = jnp.concatenate(windows, 3).reshape(slab_z * slab_x * span_y, -1)
    summed = jnp.dot(
        columns,
        weight.reshape(-1, weight.shape[2]),
        precision=lax.Precision.HIGH,
        preferred_element_type=jnp.float32,
    )
    return summed.reshape(slab_z, slab_x, span_y, weight.shape[2])


def general(features, block_mask, near_kernel_weight, far_kernel_weight):
    near_taps = reach(features, NEAR_DILATION)
    far_taps = reach(features, FAR_DILATION)
    active = jnp.repeat(jnp.repeat(jnp.repeat(block_mask, B, 0), B, 1), B, 2)
    active = active.astype(jnp.float32)[..., None]
    near_weight = gathered(near_kernel_weight, near_taps)
    far_weight = gathered(far_kernel_weight, far_taps)
    masked = active * features
    hidden = active * jnp.maximum(
        dilated_result(masked, near_weight, near_taps, NEAR_DILATION), 0.0
    )
    return active * (masked + dilated_result(hidden, far_weight, far_taps, FAR_DILATION))


def section_kernel(
    n, deep, span_y, near_step, far_step,
    feat, mask, near, far, out,
    wall, raw, stage, xs, ms, mf, xc, xl, xh, acc, hc,
    line_send, pair_send, core_send, line_recv, pair_recv, core_recv,
    x_send, x_recv, m_send, m_recv, r_send, r_recv, load_sem, own_sem,
):
    taps, wide, channels = wall.shape
    part = near.shape[1]
    half = part // 2
    positions = wide // part
    line = positions // 2
    rows = xs.shape[1]
    plane = rows // deep
    skip = plane * NEAR_DILATION // span_y
    edge = plane - skip
    side = deep * edge
    near_taps = 9

    g = lax.axis_index("gz")
    s = lax.axis_index("xy")
    pos, col = s // 2, s % 2
    core = g % 2
    twin = g + 1 - 2 * core
    mate = s + 1 - 2 * col

    home = pl.ds(pl.multiple_of(s * part, part), part)
    loads = []
    for a in range(3):
        loads.append((near.at[pl.ds(9 * a + 3, 3)], wall.at[pl.ds(3 * a, 3), home, :]))
    for a in range(3):
        loads.append((far.at[pl.ds(9 * a + 4, 1)], wall.at[pl.ds(near_taps + a, 1), home, :]))
    loads.append((feat, raw))
    loads = [pltpu.make_async_copy(a, b, load_sem.at[i]) for i, (a, b) in enumerate(loads)]
    for load in loads:
        load.start()

    barrier = pltpu.get_barrier_semaphore()
    for i in range(1, n):
        pl.semaphore_signal(barrier, inc=1, device_id={"gz": (g + i) % n}, device_id_type=MESH)
    pl.semaphore_signal(barrier, inc=1, device_id={"xy": mate}, device_id_type=MESH)

    for i in range(1, line):
        pl.semaphore_signal(barrier, inc=1, device_id={"xy": 2 * ((pos + i) % line) + col}, device_id_type=MESH)

    ms[g] = mask[g]
    for load in loads[:-1]:
        load.wait()
    pl.semaphore_wait(barrier, n + line - 1)

    def piece(p, q, h, grp):
        start = pl.multiple_of((2 * p + q) * part + h * half, half)
        return wall.at[tap_of(grp), pl.ds(start, half), :]

    def along(k, grp):
        ref = piece(pos, col, core, grp)
        where = 2 * ((pos + k) % line) + col
        return pltpu.make_async_remote_copy(
            ref, ref, line_send.at[k, grp], line_recv.at[pos, grp], device_id={"xy": where}, device_id_type=MESH)

    def from_line(p, grp):
        ref = piece(p, col, core, grp)
        return pltpu.make_async_remote_copy(
            ref, ref, line_send.at[0, grp], line_recv.at[p, grp], device_id={"xy": 2 * p + col}, device_id_type=MESH)

    def across(p, q, grp):
        ref = piece(p, q, core, grp)
        return pltpu.make_async_remote_copy(
            ref, ref, pair_send.at[p, grp], pair_recv.at[p, grp], device_id={"xy": mate}, device_id_type=MESH)

    def to_twin(p, q, h, grp):
        ref = piece(p, q, h, grp)
        where = 2 * p + q
        return pltpu.make_async_remote_copy(
            ref, ref, core_send.at[where, grp], core_recv.at[where, grp], device_id={"gz": twin}, device_id_type=MESH)

    others = [(pos + k) % line for k in range(1, line)]

    def line_stage(grp):
        for p in others:
            from_line(p, grp).wait_recv()
            across(p, col, grp).start()
            to_twin(p, col, core, grp).start()

    def pair_stage(grp):
        for p in [pos] + others:
            across(p, 1 - col, grp).wait_recv()
            to_twin(p, 1 - col, core, grp).start()

    def core_stage(grp):
        for p in others:
            to_twin(p, col, 1 - core, grp).wait_recv()
        for p in [pos] + others:
            to_twin(p, 1 - col, 1 - core, grp).wait_recv()

    def finish(grp):
        for k in range(1, line):
            along(k, grp).wait_send()
        for p in [pos] + others:
            across(p, col, grp).wait_send()
            to_twin(p, 1 - col, core, grp).wait_send()
        for p in others:
            to_twin(p, col, core, grp).wait_send()

    low = g < n // 2

    def tap_of(grp):
        return grp if grp < near_taps else jnp.where(low, grp, near_taps + taps - 1 - grp)

    def exchange(src, dst, send, recv, d):
        return pltpu.make_async_remote_copy(
            src.at[d], dst.at[g], send.at[d], recv.at[g], device_id={"gz": d}, device_id_type=MESH)

    def arrival(dst, send, recv, d):
        return pltpu.make_async_remote_copy(
            dst.at[d], dst.at[d], send.at[d], recv.at[d], device_id={"gz": d}, device_id_type=MESH)

    def split(value, ref, start, count):
        high = value.astype(jnp.bfloat16)
        low = (value - high.astype(jnp.float32)).astype(jnp.bfloat16)
        at = pl.ds(start, count)
        ref[at, 0:channels] = high
        ref[at, channels : 2 * channels] = low
        ref[at, 2 * channels :] = high

    def tap_weight(tap):
        value = wall[tap]
        high = value.astype(jnp.bfloat16)
        low = (value - high.astype(jnp.float32)).astype(jnp.bfloat16)
        return jnp.concatenate([high, high, low], axis=1)

    def product(lhs, weight):
        return lax.dot_general(lhs, weight, (((1,), (1,)), ((), ())), preferred_element_type=jnp.float32)

    def spread(source, ref, i):
        for z in range(deep):
            column = source[:plane, i * 8 + z : i * 8 + z + 1]
            ref[i * rows + z * plane : i * rows + (z + 1) * plane, :] = jnp.broadcast_to(column, (plane, 128))

    def flags_of(ref):
        flags = [ref[i] for i in range(n)]
        flags.append(jnp.zeros((128 - n * 8, 128), jnp.float32))
        return jnp.transpose(jnp.concatenate(flags, axis=0))

    def keep(at):
        return jnp.concatenate([mf[at]] * (channels // 128), axis=1)

    def mask_features(d):
        for z in range(deep):
            value = raw[d * deep + z].reshape(plane, channels)
            at = pl.ds(pl.multiple_of(d * rows + z * plane, 8), plane)
            stage[d, z * plane : (z + 1) * plane] = value * keep(at)

    def near_tap(tap):
        a, c = tap // 3 - 1, tap % 3 - 1
        first, last = max(0, a * near_step), min(n, n + a * near_step)
        if first >= last:
            return
        weight = tap_weight(tap)
        to = first - a * near_step
        if c == 0:
            acc[to * rows : (to + last - first) * rows] += product(xc[first * rows : last * rows], weight)
        else:
            source, offset = (xl, skip) if c < 0 else (xh, 0)
            result = product(source[first * side : last * side], weight)
            for i in range((last - first) * deep):
                base = to * rows + i * plane + offset
                acc[base : base + edge] += result[i * edge : (i + 1) * edge]

    def far_tap(tap):
        a = tap - near_taps - 1
        first, last = max(0, a * far_step), min(n, n + a * far_step)
        if first >= last:
            return
        to = first - a * far_step
        acc[to * rows : (to + last - first) * rows] += product(hc[first * rows : last * rows], tap_weight(tap))

    def give(i):
        d = (g + i) % n
        at = pl.ds(pl.multiple_of(d * rows, rows), rows)
        exchange(stage, xs, x_send, x_recv, d).wait_send()
        stage[d] = acc[at] * keep(at)
        exchange(stage, out, r_send, r_recv, d).start()

    def far_stage(grp):
        order = grp - near_taps

        @pl.when(low)
        def _():
            far_tap(near_taps + order)
            if order == 1:
                for d in range(n // 2, n):
                    give(d - g)

        @pl.when(jnp.logical_not(low))
        def _():
            far_tap(near_taps + 2 - order)
            if order == 1:
                for d in range(n // 2):
                    give(d + n - g)

    def turn():
        for i in range(n):
            at = slice(i * rows, (i + 1) * rows)
            value = jnp.maximum(acc[at], 0.0) * keep(at)
            split(value, hc, i * rows, rows)
            acc[at] = xs[i]

    def take_features():
        for i in range(1, n):
            d = (g + i) % n
            arrival(xs, x_send, x_recv, d).wait_recv()
            arrival(ms, m_send, m_recv, d).wait_recv()
        flags = flags_of(ms)
        for i in range(n):
            value = xs[i]
            split(value, xc, i * rows, rows)
            planes = [value[z * plane : (z + 1) * plane] for z in range(deep)]
            split(jnp.concatenate([one[:edge] for one in planes], axis=0), xl, i * side, side)
            split(jnp.concatenate([one[skip:] for one in planes], axis=0), xh, i * side, side)
            spread(flags, mf, i)
        acc[...] = jnp.zeros_like(acc)

    def compute(grp):
        if grp == 0:
            take_features()
        if grp < near_taps:
            near_tap(grp)
            if grp == near_taps - 1:
                turn()
        else:
            far_stage(grp)

    for grp in range(taps):
        for k in range(1, line):
            along(k, grp).start()
        across(pos, col, grp).start()
    flags = flags_of(mask)
    for i in range(n):
        spread(flags, mf, i)
    loads[-1].wait()
    half_way = n // 2
    near_by = [i for i in range(1, n) if i != half_way]
    for i in [half_way] + near_by:
        d = (g + i) % n
        mask_features(d)
        exchange(stage, xs, x_send, x_recv, d).start()
        exchange(mask, ms, m_send, m_recv, d).start()
    mask_features(g)
    xs[g] = stage[g]

    for tau in range(taps + 2):
        if tau < taps:
            line_stage(tau)
        if 0 <= tau - 1 < taps:
            pair_stage(tau - 1)
        if 0 <= tau - 2:
            core_stage(tau - 2)
            compute(tau - 2)

    for i in range(1, n // 2):
        give((g // (n // 2)) * (n // 2) + (g + i) % (n // 2) + n - g)
    at = pl.ds(pl.multiple_of(g * rows, rows), rows)
    stage[g] = acc[at] * keep(at)
    own = pltpu.make_async_copy(stage.at[g], out.at[g], own_sem)
    own.start()
    for grp in range(taps):
        finish(grp)
    own.wait()
    for i in range(1, n):
        d = (g + i) % n
        exchange(mask, ms, m_send, m_recv, d).wait_send()
        exchange(stage, out, r_send, r_recv, d).wait_send()
        arrival(out, r_send, r_recv, d).wait_recv()


def fits(features, weight):
    slab_z, slab_x, span_y, channels = features.shape
    n, m = lax.axis_size("gz"), lax.axis_size("xy")
    deep, plane, part = slab_z // n, span_y * slab_x, weight.shape[2]
    return (
        FAR_DILATION >= span_y > NEAR_DILATION
        and NEAR_DILATION >= slab_x * m
        and NEAR_DILATION % slab_z == 0 and FAR_DILATION % slab_z == 0
        and n % 2 == 0 and 2 * FAR_DILATION >= n * slab_z and m % 2 == 0 and m >= 4
        and slab_z % n == 0 and deep <= 8 and n <= 16
        and plane <= 128 and plane % 8 == 0 and NEAR_DILATION * slab_x % 8 == 0
        and deep * plane % 16 == 0 and deep * (span_y - NEAR_DILATION) * slab_x % 16 == 0
        and channels % 128 == 0 and part % 16 == 0 and part * m == channels
    )


def fast(features, block_mask, near_kernel_weight, far_kernel_weight):
    slab_z, slab_x, span_y, channels = features.shape
    n, m = lax.axis_size("gz"), lax.axis_size("xy")
    part = near_kernel_weight.shape[2]
    deep, plane = slab_z // n, span_y * slab_x
    rows, side = deep * plane, deep * (span_y - NEAR_DILATION) * slab_x
    near = jnp.swapaxes(near_kernel_weight, 1, 2)
    far = jnp.swapaxes(far_kernel_weight, 1, 2)
    active = jnp.repeat(jnp.repeat(jnp.repeat(block_mask, B, 0), B, 1), B, 2).astype(jnp.float32)
    active = jnp.swapaxes(active, 1, 2)
    feat = jnp.swapaxes(features, 1, 2)
    mask = jnp.pad(active.reshape(n, deep, plane), ((0, 0), (0, 8 - deep), (0, 128 - plane)))
    taps = 12
    groups, line = taps, m // 2
    dma = pltpu.SemaphoreType.DMA
    vmem, hbm = pl.BlockSpec(memory_space=pltpu.VMEM), pl.BlockSpec(memory_space=pl.ANY)
    out = pl.pallas_call(
        functools.partial(section_kernel, n, deep, span_y, NEAR_DILATION // slab_z, FAR_DILATION // slab_z),
        out_shape=jax.ShapeDtypeStruct((n, rows, channels), jnp.float32),
        in_specs=[hbm, vmem, hbm, hbm],
        out_specs=hbm,
        scratch_shapes=[
            pltpu.VMEM((taps, m * part, channels), jnp.float32),
            pltpu.VMEM(feat.shape, jnp.float32),
            pltpu.VMEM((n, rows, channels), jnp.float32),
            pltpu.VMEM((n, rows, channels), jnp.float32),
            pltpu.VMEM((n, 8, 128), jnp.float32),
            pltpu.VMEM((n * rows, 128), jnp.float32),
            pltpu.VMEM((n * rows, 3 * channels), jnp.bfloat16),
            pltpu.VMEM((n * side, 3 * channels), jnp.bfloat16),
            pltpu.VMEM((n * side, 3 * channels), jnp.bfloat16),
            pltpu.VMEM((n * rows, channels), jnp.float32),
            pltpu.VMEM((n * rows, 3 * channels), jnp.bfloat16),
            dma((line, groups)), dma((line, groups)), dma((m, groups)),
            dma((line, groups)), dma((line, groups)), dma((m, groups)),
            dma((n,)), dma((n,)), dma((n,)), dma((n,)), dma((n,)), dma((n,)), dma((7,)), dma,
        ],
        compiler_params=pltpu.CompilerParams(
            collective_id=0, has_side_effects=True, vmem_limit_bytes=60 * 1024 * 1024),
        cost_estimate=pl.CostEstimate(flops=3 * 10**9, bytes_accessed=4 * 10**6, transcendentals=0),
    )(feat, mask, near, far)
    return jnp.swapaxes(out.reshape(slab_z, span_y, slab_x, channels), 1, 2)


def local(features, block_mask, near_kernel_weight, far_kernel_weight):
    form = fast if fits(features, near_kernel_weight) else general
    return form(features, block_mask, near_kernel_weight, far_kernel_weight)


def solution(mesh):
    in_specs = (
        P("gz", "xy", None, None),
        P("gz", "xy", None),
        P(None, None, "xy"),
        P(None, None, "xy"),
    )
    out_specs = P("gz", "xy", None, None)
    return jax.shard_map(local, mesh=mesh, in_specs=in_specs, out_specs=out_specs, check_vma=False)
```

```python
import functools

import jax
import jax.numpy as jnp
from jax import lax
from jax.experimental import pallas as pl
from jax.experimental.pallas import tpu as pltpu
from jax.sharding import PartitionSpec as P

B = 2
NEAR_DILATION = 16
FAR_DILATION = 32
WINDOW = 4
MESH = pl.DeviceIdType.MESH


def offsets(dilation, extent):
    return (-1, 0, 1) if dilation < extent else (0,)


def from_behind(block, axis, distance):
    if distance == 0:
        return block
    devices = range(lax.axis_size(axis))
    route = [(i - distance, i) for i in devices if i - distance in devices]
    return lax.ppermute(block, axis, route)


def reach(field, dilation):
    slab_z, slab_x, span_y, _ = field.shape
    return (
        offsets(dilation, slab_z * lax.axis_size("gz")),
        offsets(dilation, slab_x * lax.axis_size("xy")),
        offsets(dilation, span_y),
    )


def gathered(weight, taps):
    cube = weight.reshape((3, 3, 3) + weight.shape[1:])
    for dim, tap in enumerate(taps):
        cube = cube if len(tap) == 3 else lax.slice_in_dim(cube, 1, 2, axis=dim)
    flat = cube.reshape((-1,) + weight.shape[1:])
    return lax.all_gather(flat, "xy", axis=2, tiled=True)


def dilated_result(field, weight, taps, dilation):
    slab_z, slab_x, span_y, channels = field.shape
    windows = []
    for a in taps[0]:
        over_z = from_behind(field, "gz", -a * dilation // slab_z)
        for b in taps[1]:
            over_x = from_behind(over_z, "xy", -b * dilation // slab_x)
            for c in taps[2]:
                if c == 0:
                    windows.append(over_x)
                elif c < 0:
                    part = over_x[:, :, : span_y - dilation]
                    windows.append(jnp.pad(part, ((0, 0), (0, 0), (dilation, 0), (0, 0))))
                else:
                    part = over_x[:, :, dilation:]
                    windows.append(jnp.pad(part, ((0, 0), (0, 0), (0, dilation), (0, 0))))
    columns = jnp.concatenate(windows, 3).reshape(slab_z * slab_x * span_y, -1)
    summed = jnp.dot(
        columns,
        weight.reshape(-1, weight.shape[2]),
        precision=lax.Precision.HIGH,
        preferred_element_type=jnp.float32,
    )
    return summed.reshape(slab_z, slab_x, span_y, weight.shape[2])


def general(features, block_mask, near_kernel_weight, far_kernel_weight):
    near_taps = reach(features, NEAR_DILATION)
    far_taps = reach(features, FAR_DILATION)
    active = jnp.repeat(jnp.repeat(jnp.repeat(block_mask, B, 0), B, 1), B, 2)
    active = active.astype(jnp.float32)[..., None]
    near_weight = gathered(near_kernel_weight, near_taps)
    far_weight = gathered(far_kernel_weight, far_taps)
    masked = active * features
    hidden = active * jnp.maximum(
        dilated_result(masked, near_weight, near_taps, NEAR_DILATION), 0.0
    )
    return active * (masked + dilated_result(hidden, far_weight, far_taps, FAR_DILATION))


def section_kernel(
    n, deep, span_y, near_step, far_step,
    feat, mask, near, far, out,
    wall, raw, raw_mask, stage, back, xs, ms, mf, xc, xl, xh, acc, hc,
    line_send, pair_send, core_send, line_recv, pair_recv, core_recv,
    x_send, x_recv, m_send, m_recv, r_send, r_recv, load_sem, out_sem,
):
    taps, _, _, line, half, channels = wall.shape
    slab_x = raw.shape[2]
    rows = xs.shape[1]
    plane = rows // deep
    skip = plane * NEAR_DILATION // span_y
    edge = plane - skip
    side = deep * edge
    near_taps = 9

    g = lax.axis_index("gz")
    s = lax.axis_index("xy")
    pos, col = s // 2, s % 2
    core = g % 2
    twin = g + 1 - 2 * core
    mate = s + 1 - 2 * col

    loads = [(mask, raw_mask), (feat, raw)]
    rows_of = pl.ds(pl.multiple_of(core * half, half), half)
    for a in range(3):
        loads.append((near.at[pl.ds(9 * a + 3, 3), rows_of], wall.at[pl.ds(3 * a, 3), core, col, pos]))
    for a in range(3):
        loads.append((far.at[9 * a + 4, rows_of], wall.at[near_taps + a, core, col, pos]))
    loads = [pltpu.make_async_copy(a, b, load_sem.at[i]) for i, (a, b) in enumerate(loads)]
    for load in loads:
        load.start()

    barrier = pltpu.get_barrier_semaphore()
    for i in range(1, n):
        pl.semaphore_signal(barrier, inc=1, device_id={"gz": (g + i) % n}, device_id_type=MESH)
    pl.semaphore_signal(barrier, inc=1, device_id={"xy": mate}, device_id_type=MESH)

    for i in range(1, line):
        pl.semaphore_signal(barrier, inc=1, device_id={"xy": 2 * ((pos + i) % line) + col}, device_id_type=MESH)

    for load in loads[2:]:
        load.wait()
    pl.semaphore_wait(barrier, n + line - 1)

    def along(k, grp):
        ref = wall.at[tap_of(grp), core, col, pos]
        where = 2 * ((pos + k) % line) + col
        return pltpu.make_async_remote_copy(
            ref, ref, line_send.at[k, grp], line_recv.at[pos, grp], device_id={"xy": where}, device_id_type=MESH)

    def from_line(p, grp):
        ref = wall.at[tap_of(grp), core, col, p]
        return pltpu.make_async_remote_copy(
            ref, ref, line_send.at[0, grp], line_recv.at[p, grp], device_id={"xy": 2 * p + col}, device_id_type=MESH)

    def across(q, grp):
        ref = wall.at[tap_of(grp), core, q]
        return pltpu.make_async_remote_copy(
            ref, ref, pair_send.at[grp], pair_recv.at[grp], device_id={"xy": mate}, device_id_type=MESH)

    def to_twin(h, grp):
        ref = wall.at[tap_of(grp), h]
        return pltpu.make_async_remote_copy(
            ref, ref, core_send.at[grp], core_recv.at[grp], device_id={"gz": twin}, device_id_type=MESH)

    def line_start(grp):
        for k in range(1, line):
            along(k, grp).start()

    def line_stage(grp):
        for k in range(1, line):
            from_line((pos + k) % line, grp).wait_recv()
        across(col, grp).start()

    def pair_stage(grp):
        across(1 - col, grp).wait_recv()
        to_twin(core, grp).start()

    def core_stage(grp):
        to_twin(1 - core, grp).wait_recv()

    def finish(grp):
        for k in range(1, line):
            along(k, grp).wait_send()
        across(col, grp).wait_send()
        to_twin(core, grp).wait_send()

    low = g < n // 2

    def tap_of(grp):
        return grp if grp < near_taps else jnp.where(low, grp, near_taps + taps - 1 - grp)

    def exchange(src, dst, send, recv, d):
        return pltpu.make_async_remote_copy(
            src.at[d], dst.at[g], send.at[d], recv.at[g], device_id={"gz": d}, device_id_type=MESH)

    def toward(d):
        return pltpu.make_async_remote_copy(
            ms.at[g], ms.at[g], m_send.at[d], m_recv.at[g], device_id={"gz": d}, device_id_type=MESH)

    def arrival(dst, send, recv, d):
        return pltpu.make_async_remote_copy(
            dst.at[d], dst.at[d], send.at[d], recv.at[d], device_id={"gz": d}, device_id_type=MESH)

    def split(value, ref, start, count):
        high = value.astype(jnp.bfloat16)
        low = (value - high.astype(jnp.float32)).astype(jnp.bfloat16)
        at = pl.ds(start, count)
        ref[at, 0:channels] = high
        ref[at, channels : 2 * channels] = low
        ref[at, 2 * channels :] = high

    def tap_weight(tap):
        value = jnp.concatenate([wall[tap, h, q, p] for p in range(line) for q in range(2) for h in range(2)], axis=0)
        high = value.astype(jnp.bfloat16)
        low = (value - high.astype(jnp.float32)).astype(jnp.bfloat16)
        return jnp.concatenate([high, high, low], axis=1)

    def product(lhs, weight):
        return lax.dot_general(lhs, weight, (((1,), (1,)), ((), ())), preferred_element_type=jnp.float32)

    def columns(ref, picks):
        chosen = [ref[slab, pl.ds(row, 1), :] for slab, row in picks]
        chosen.append(jnp.zeros((-len(picks) % 8 + 8, 128), jnp.float32))
        r = lax.broadcasted_iota(jnp.int32, (plane, 128), 0)
        k = lax.broadcasted_iota(jnp.int32, (plane, 128), 1)
        block = (r % slab_x) // B * (span_y // B) + r // slab_x // B
        return product((block == k).astype(jnp.float32), jnp.concatenate(chosen, axis=0))

    def spread(flags, i):
        for z in range(deep):
            at = i * (deep // B) + z // B
            column = flags[:, at : at + 1]
            mf[i * rows + z * plane : i * rows + (z + 1) * plane, :] = jnp.broadcast_to(column, (plane, 128))

    def keep(at):
        return jnp.concatenate([mf[at]] * (channels // 128), axis=1)

    def mask_features(d):
        for z in range(deep):
            value = raw[d * deep + z].reshape(plane, channels)
            at = pl.ds(pl.multiple_of(d * rows + z * plane, 8), plane)
            stage[d, z * plane : (z + 1) * plane] = value * keep(at)

    def near_tap(tap):
        a, c = tap // 3 - 1, tap % 3 - 1
        first, last = max(0, a * near_step), min(n, n + a * near_step)
        if first >= last:
            return
        weight = tap_weight(tap)
        to = first - a * near_step
        if c == 0:
            acc[to * rows : (to + last - first) * rows] += product(xc[first * rows : last * rows], weight)
        else:
            source, offset = (xl, skip) if c < 0 else (xh, 0)
            result = product(source[first * side : last * side], weight)
            for i in range((last - first) * deep):
                base = to * rows + i * plane + offset
                acc[base : base + edge] += result[i * edge : (i + 1) * edge]

    def far_tap(tap):
        a = tap - near_taps - 1
        first, last = max(0, a * far_step), min(n, n + a * far_step)
        if first >= last:
            return
        to = first - a * far_step
        acc[to * rows : (to + last - first) * rows] += product(hc[first * rows : last * rows], tap_weight(tap))

    def give(i):
        d = (g + i) % n
        at = pl.ds(pl.multiple_of(d * rows, rows), rows)
        exchange(stage, xs, x_send, x_recv, d).wait_send()
        stage[d] = acc[at] * keep(at)
        exchange(stage, back, r_send, r_recv, d).start()

    def far_stage(grp):
        order = grp - near_taps

        @pl.when(low)
        def _():
            far_tap(near_taps + order)
            if order == 1:
                for d in range(n // 2, n):
                    give(d - g)

        @pl.when(jnp.logical_not(low))
        def _():
            far_tap(near_taps + 2 - order)
            if order == 1:
                for d in range(n // 2):
                    give(d + n - g)

    def turn():
        for i in range(n):
            at = slice(i * rows, (i + 1) * rows)
            value = jnp.maximum(acc[at], 0.0) * keep(at)
            split(value, hc, i * rows, rows)
            acc[at] = xs[i]

    def take_features():
        for i in range(1, n):
            d = (g + i) % n
            arrival(xs, x_send, x_recv, d).wait_recv()
            arrival(ms, m_send, m_recv, d).wait_recv()
        flags = columns(ms, [(i, g * (deep // B) + j) for i in range(n) for j in range(deep // B)])
        for i in range(n):
            value = xs[i]
            split(value, xc, i * rows, rows)
            planes = [value[z * plane : (z + 1) * plane] for z in range(deep)]
            split(jnp.concatenate([one[:edge] for one in planes], axis=0), xl, i * side, side)
            split(jnp.concatenate([one[skip:] for one in planes], axis=0), xh, i * side, side)
            spread(flags, i)
        acc[...] = jnp.zeros_like(acc)

    def compute(grp):
        if grp == 0:
            take_features()
        if grp < near_taps:
            near_tap(grp)
            if grp == near_taps - 1:
                turn()
        else:
            far_stage(grp)

    for grp in range(WINDOW):
        line_start(grp)
    for load in loads[:2]:
        load.wait()
    ms[g] = jnp.zeros((ms.shape[1], 128), jnp.float32)
    for x in range(raw_mask.shape[1]):
        value = raw_mask[:, x, :].astype(jnp.float32)
        ms[g, :, x * (span_y // B) : (x + 1) * (span_y // B)] = value
    flags = columns(ms, [(g, j) for j in range(n * deep // B)])
    for i in range(n):
        spread(flags, i)
    half_way = n // 2
    near_by = [i for i in range(1, n) if i != half_way]
    for i in [half_way] + near_by:
        d = (g + i) % n
        mask_features(d)
        exchange(stage, xs, x_send, x_recv, d).start()
        toward(d).start()
    mask_features(g)
    xs[g] = stage[g]

    for tau in range(taps + 2):
        if tau < taps:
            line_stage(tau)
            if tau + WINDOW < taps:
                line_start(tau + WINDOW)
        if 0 <= tau - 1 < taps:
            pair_stage(tau - 1)
        if 0 <= tau - 2:
            core_stage(tau - 2)
            compute(tau - 2)

    for i in range(1, n // 2):
        give((g // (n // 2)) * (n // 2) + (g + i) % (n // 2) + n - g)
    def deliver(d, source):
        for z in range(deep):
            raw[d * deep + z] = source[z * plane : (z + 1) * plane].reshape(raw.shape[1:])
        return pltpu.make_async_copy(raw.at[pl.ds(d * deep, deep)], out.at[pl.ds(d * deep, deep)], out_sem.at[d])

    at = pl.ds(pl.multiple_of(g * rows, rows), rows)
    deliver(g, acc[at] * keep(at)).start()
    for grp in range(taps):
        finish(grp)
    for i in range(1, n):
        d = (g + i) % n
        toward(d).wait_send()
        exchange(stage, back, r_send, r_recv, d).wait_send()
    for i in near_by + [half_way]:
        d = (g + i) % n
        arrival(back, r_send, r_recv, d).wait_recv()
        deliver(d, back[d]).start()
    for d in range(n):
        pltpu.make_async_copy(raw.at[pl.ds(d * deep, deep)], out.at[pl.ds(d * deep, deep)], out_sem.at[d]).wait()


def fits(features, weight):
    slab_z, slab_x, span_y, channels = features.shape
    n, m = lax.axis_size("gz"), lax.axis_size("xy")
    deep, plane, part = slab_z // n, span_y * slab_x, weight.shape[2]
    return (
        FAR_DILATION >= span_y > NEAR_DILATION
        and NEAR_DILATION >= slab_x * m
        and NEAR_DILATION % slab_z == 0 and FAR_DILATION % slab_z == 0
        and n % 4 == 0 and 2 * FAR_DILATION >= n * slab_z and m % 2 == 0 and m >= 4
        and slab_z % (B * n) == 0 and slab_x % B == 0 and span_y % B == 0 and slab_z // B % 8 == 0
        and plane <= 128 and plane % 8 == 0 and NEAR_DILATION * slab_x % 8 == 0
        and deep * plane % 16 == 0 and deep * (span_y - NEAR_DILATION) * slab_x % 16 == 0
        and channels % 128 == 0 and part % 16 == 0 and part * m == channels
    )


def fast(features, block_mask, near_kernel_weight, far_kernel_weight):
    slab_z, slab_x, span_y, channels = features.shape
    n, m = lax.axis_size("gz"), lax.axis_size("xy")
    part = near_kernel_weight.shape[2]
    deep, plane = slab_z // n, span_y * slab_x
    rows, side = deep * plane, deep * (span_y - NEAR_DILATION) * slab_x
    near = jnp.swapaxes(near_kernel_weight, 1, 2)
    far = jnp.swapaxes(far_kernel_weight, 1, 2)
    feat = jnp.swapaxes(features, 1, 2)
    taps = 12
    line = m // 2
    dma = pltpu.SemaphoreType.DMA
    hbm = pl.BlockSpec(memory_space=pl.ANY)
    out = pl.pallas_call(
        functools.partial(section_kernel, n, deep, span_y, NEAR_DILATION // slab_z, FAR_DILATION // slab_z),
        out_shape=jax.ShapeDtypeStruct(feat.shape, jnp.float32),
        in_specs=[hbm] * 4,
        out_specs=hbm,
        scratch_shapes=[
            pltpu.VMEM((taps, 2, 2, line, part // 2, channels), jnp.float32),
            pltpu.VMEM(feat.shape, jnp.float32),
            pltpu.VMEM(block_mask.shape, jnp.int32),
            pltpu.VMEM((n, rows, channels), jnp.float32),
            pltpu.VMEM((n, rows, channels), jnp.float32),
            pltpu.VMEM((n, rows, channels), jnp.float32),
            pltpu.VMEM((n, slab_z // B, 128), jnp.float32),
            pltpu.VMEM((n * rows, 128), jnp.float32),
            pltpu.VMEM((n * rows, 3 * channels), jnp.bfloat16),
            pltpu.VMEM((n * side, 3 * channels), jnp.bfloat16),
            pltpu.VMEM((n * side, 3 * channels), jnp.bfloat16),
            pltpu.VMEM((n * rows, channels), jnp.float32),
            pltpu.VMEM((n * rows, 3 * channels), jnp.bfloat16),
            dma((line, taps)), dma((taps,)), dma((taps,)),
            dma((line, taps)), dma((taps,)), dma((taps,)),
            dma((n,)), dma((n,)), dma((n,)), dma((n,)), dma((n,)), dma((n,)), dma((8,)), dma((n,)),
        ],
        compiler_params=pltpu.CompilerParams(
            collective_id=0, has_side_effects=True, vmem_limit_bytes=60 * 1024 * 1024),
        cost_estimate=pl.CostEstimate(flops=3 * 10**9, bytes_accessed=4 * 10**6, transcendentals=0),
    )(feat, block_mask, near, far)
    return jnp.swapaxes(out, 1, 2)


def local(features, block_mask, near_kernel_weight, far_kernel_weight):
    form = fast if fits(features, near_kernel_weight) else general
    return form(features, block_mask, near_kernel_weight, far_kernel_weight)


def solution(mesh):
    in_specs = (
        P("gz", "xy", None, None),
        P("gz", "xy", None),
        P(None, None, "xy"),
        P(None, None, "xy"),
    )
    out_specs = P("gz", "xy", None, None)
    return jax.shard_map(local, mesh=mesh, in_specs=in_specs, out_specs=out_specs, check_vma=False)
```

```python
import functools

import jax
import jax.numpy as jnp
from jax import lax
from jax.experimental import pallas as pl
from jax.experimental.pallas import tpu as pltpu
from jax.sharding import PartitionSpec as P

B = 2
NEAR_DILATION = 16
FAR_DILATION = 32
WINDOW = 4
LEAD = 9
MESH = pl.DeviceIdType.MESH


def offsets(dilation, extent):
    return (-1, 0, 1) if dilation < extent else (0,)


def from_behind(block, axis, distance):
    if distance == 0:
        return block
    devices = range(lax.axis_size(axis))
    route = [(i - distance, i) for i in devices if i - distance in devices]
    return lax.ppermute(block, axis, route)


def reach(field, dilation):
    slab_z, slab_x, span_y, _ = field.shape
    return (
        offsets(dilation, slab_z * lax.axis_size("gz")),
        offsets(dilation, slab_x * lax.axis_size("xy")),
        offsets(dilation, span_y),
    )


def gathered(weight, taps):
    cube = weight.reshape((3, 3, 3) + weight.shape[1:])
    for dim, tap in enumerate(taps):
        cube = cube if len(tap) == 3 else lax.slice_in_dim(cube, 1, 2, axis=dim)
    flat = cube.reshape((-1,) + weight.shape[1:])
    return lax.all_gather(flat, "xy", axis=2, tiled=True)


def dilated_result(field, weight, taps, dilation):
    slab_z, slab_x, span_y, channels = field.shape
    windows = []
    for a in taps[0]:
        over_z = from_behind(field, "gz", -a * dilation // slab_z)
        for b in taps[1]:
            over_x = from_behind(over_z, "xy", -b * dilation // slab_x)
            for c in taps[2]:
                if c == 0:
                    windows.append(over_x)
                elif c < 0:
                    part = over_x[:, :, : span_y - dilation]
                    windows.append(jnp.pad(part, ((0, 0), (0, 0), (dilation, 0), (0, 0))))
                else:
                    part = over_x[:, :, dilation:]
                    windows.append(jnp.pad(part, ((0, 0), (0, 0), (0, dilation), (0, 0))))
    columns = jnp.concatenate(windows, 3).reshape(slab_z * slab_x * span_y, -1)
    summed = jnp.dot(
        columns,
        weight.reshape(-1, weight.shape[2]),
        precision=lax.Precision.HIGH,
        preferred_element_type=jnp.float32,
    )
    return summed.reshape(slab_z, slab_x, span_y, weight.shape[2])


def general(features, block_mask, near_kernel_weight, far_kernel_weight):
    near_taps = reach(features, NEAR_DILATION)
    far_taps = reach(features, FAR_DILATION)
    active = jnp.repeat(jnp.repeat(jnp.repeat(block_mask, B, 0), B, 1), B, 2)
    active = active.astype(jnp.float32)[..., None]
    near_weight = gathered(near_kernel_weight, near_taps)
    far_weight = gathered(far_kernel_weight, far_taps)
    masked = active * features
    hidden = active * jnp.maximum(
        dilated_result(masked, near_weight, near_taps, NEAR_DILATION), 0.0
    )
    return active * (masked + dilated_result(hidden, far_weight, far_taps, FAR_DILATION))


def section_kernel(
    n, deep, span_y, near_step, far_step,
    feat, mask, near, far, out,
    wall, raw, raw_mask, stage, back, xs, ms, mf, xc, xl, xh, acc, hc, total,
    line_send, pair_send, core_send, line_recv, pair_recv, core_recv,
    x_send, x_recv, m_send, m_recv, r_send, r_recv, load_sem, out_sem,
):
    taps, _, _, line, half, channels = wall.shape
    slab_x = raw.shape[2]
    rows = xs.shape[1]
    plane = rows // deep
    skip = plane * NEAR_DILATION // span_y
    edge = plane - skip
    side = deep * edge
    near_taps = 9

    g = lax.axis_index("gz")
    s = lax.axis_index("xy")
    pos, col = s // 2, s % 2
    core = g % 2
    twin = g + 1 - 2 * core
    mate = s + 1 - 2 * col

    loads = [(mask, raw_mask), (feat, raw)]
    rows_of = pl.ds(pl.multiple_of(core * half, half), half)
    for a in range(3):
        loads.append((near.at[pl.ds(9 * a + 3, 3), rows_of], wall.at[pl.ds(3 * a, 3), core, col, pos]))
    for a in range(3):
        loads.append((far.at[9 * a + 4, rows_of], wall.at[near_taps + a, core, col, pos]))
    loads = [pltpu.make_async_copy(a, b, load_sem.at[i]) for i, (a, b) in enumerate(loads)]
    for load in loads:
        load.start()

    barrier = pltpu.get_barrier_semaphore()
    for i in range(1, n):
        pl.semaphore_signal(barrier, inc=1, device_id={"gz": (g + i) % n}, device_id_type=MESH)
    pl.semaphore_signal(barrier, inc=1, device_id={"xy": mate}, device_id_type=MESH)

    for i in range(1, line):
        pl.semaphore_signal(barrier, inc=1, device_id={"xy": 2 * ((pos + i) % line) + col}, device_id_type=MESH)

    for load in loads[2:]:
        load.wait()
    pl.semaphore_wait(barrier, n + line - 1)

    def along(k, grp):
        ref = wall.at[tap_of(grp), core, col, pos]
        where = 2 * ((pos + k) % line) + col
        return pltpu.make_async_remote_copy(
            ref, ref, line_send.at[k, grp], line_recv.at[pos, grp], device_id={"xy": where}, device_id_type=MESH)

    def from_line(p, grp):
        ref = wall.at[tap_of(grp), core, col, p]
        return pltpu.make_async_remote_copy(
            ref, ref, line_send.at[0, grp], line_recv.at[p, grp], device_id={"xy": 2 * p + col}, device_id_type=MESH)

    def across(q, grp):
        ref = wall.at[tap_of(grp), core, q]
        return pltpu.make_async_remote_copy(
            ref, ref, pair_send.at[grp], pair_recv.at[grp], device_id={"xy": mate}, device_id_type=MESH)

    def to_twin(h, grp):
        ref = wall.at[tap_of(grp), h]
        return pltpu.make_async_remote_copy(
            ref, ref, core_send.at[grp], core_recv.at[grp], device_id={"gz": twin}, device_id_type=MESH)

    def line_start(grp):
        for k in range(1, line):
            along(k, grp).start()

    def line_stage(grp):
        for k in range(1, line):
            from_line((pos + k) % line, grp).wait_recv()
        across(col, grp).start()

    def pair_stage(grp):
        across(1 - col, grp).wait_recv()
        to_twin(core, grp).start()

    def core_stage(grp):
        to_twin(1 - core, grp).wait_recv()

    def finish(grp):
        for k in range(1, line):
            along(k, grp).wait_send()
        across(col, grp).wait_send()
        to_twin(core, grp).wait_send()

    low = g < n // 2

    def tap_of(grp):
        return jnp.where(low | (grp < near_taps), grp, near_taps + taps - 1 - grp)

    def exchange(src, dst, send, recv, d):
        return pltpu.make_async_remote_copy(
            src.at[d], dst.at[g], send.at[d], recv.at[g], device_id={"gz": d}, device_id_type=MESH)

    def toward(d):
        return pltpu.make_async_remote_copy(
            ms.at[g], ms.at[g], m_send.at[d], m_recv.at[g], device_id={"gz": d}, device_id_type=MESH)

    def arrival(dst, send, recv, d):
        return pltpu.make_async_remote_copy(
            dst.at[d], dst.at[d], send.at[d], recv.at[d], device_id={"gz": d}, device_id_type=MESH)

    def split(value, ref, start, count):
        high = value.astype(jnp.bfloat16)
        low = (value - high.astype(jnp.float32)).astype(jnp.bfloat16)
        at = pl.ds(pl.multiple_of(start, 16), count)
        ref[at, 0:channels] = high
        ref[at, channels : 2 * channels] = low
        ref[at, 2 * channels :] = high

    def tap_weight(tap):
        value = jnp.concatenate([wall[tap, h, q, p] for p in range(line) for q in range(2) for h in range(2)], axis=0)
        high = value.astype(jnp.bfloat16)
        low = (value - high.astype(jnp.float32)).astype(jnp.bfloat16)
        return jnp.concatenate([high, high, low], axis=1)

    def product(lhs, weight):
        return lax.dot_general(lhs, weight, (((1,), (1,)), ((), ())), preferred_element_type=jnp.float32)

    def columns(ref, picks):
        chosen = [ref[slab, pl.ds(row, 1), :] for slab, row in picks]
        chosen.append(jnp.zeros((-len(picks) % 8 + 8, 128), jnp.float32))
        r = lax.broadcasted_iota(jnp.int32, (plane, 128), 0)
        k = lax.broadcasted_iota(jnp.int32, (plane, 128), 1)
        block = (r % slab_x) // B * (span_y // B) + r // slab_x // B
        return product((block == k).astype(jnp.float32), jnp.concatenate(chosen, axis=0))

    def spread(flags, i):
        for z in range(deep):
            at = i * (deep // B) + z // B
            column = flags[:, at : at + 1]
            mf[i * rows + z * plane : i * rows + (z + 1) * plane, :] = jnp.broadcast_to(column, (plane, 128))

    def keep(at):
        return jnp.concatenate([mf[at]] * (channels // 128), axis=1)

    def mask_features(d):
        for z in range(deep):
            value = raw[d * deep + z].reshape(plane, channels)
            at = pl.ds(pl.multiple_of(d * rows + z * plane, 8), plane)
            stage[d, z * plane : (z + 1) * plane] = value * keep(at)

    def slab(i):
        return pl.ds(pl.multiple_of(i * rows, rows), rows)

    def near_tap(a, c):
        weight = tap_weight(3 * a + c)
        base = pl.multiple_of((2 - a) * near_step * rows, rows)
        if c == 1:
            at = pl.ds(base, n * rows)
            acc[at] += product(xc[...], weight)
            return
        source, offset = (xl, skip) if c == 0 else (xh, 0)
        result = product(source[...], weight)
        for i in range(n * deep):
            at = pl.ds(pl.multiple_of(base + i * plane + offset, 8), edge)
            acc[at] += result[i * edge : (i + 1) * edge]

    def give(d):
        exchange(stage, xs, x_send, x_recv, d).wait_send()
        stage[d] = total[slab(d)] * keep(slab(d))
        exchange(stage, back, r_send, r_recv, d).start()

    def far_stage(order):
        weight = tap_weight(tap_of(near_taps + order))
        if order == 1:
            total[...] += product(hc[...], weight)
            return
        count = (n - far_step) * rows
        front = low if order == 0 else jnp.logical_not(low)
        source = pl.multiple_of(jnp.where(front, 0, far_step * rows), rows)
        target = pl.multiple_of(jnp.where(front, far_step * rows, 0), rows)
        total[pl.ds(target, count)] += product(hc[pl.ds(source, count)], weight)

    def turn(i, _):
        at = slab(i)
        value = jnp.maximum(acc[pl.ds(pl.multiple_of((i + near_step) * rows, rows), rows)], 0.0) * keep(at)
        split(value, hc, i * rows, rows)
        total[at] = xs[i]
        return 0

    def take_slab(i, _):
        value = xs[i]
        split(value, xc, i * rows, rows)
        planes = [value[z * plane : (z + 1) * plane] for z in range(deep)]
        split(jnp.concatenate([one[:edge] for one in planes], axis=0), xl, i * side, side)
        split(jnp.concatenate([one[skip:] for one in planes], axis=0), xh, i * side, side)
        return 0

    def step(tau):
        @pl.when(tau < taps)
        def _():
            line_stage(tau)

        @pl.when(tau + WINDOW < taps)
        def _():
            line_start(tau + WINDOW)

        @pl.when((tau >= 1) & (tau <= taps))
        def _():
            pair_stage(tau - 1)

    def finish_all(grp, _):
        finish(grp)
        return 0

    def lead(tau, _):
        step(tau)
        return 0

    def near_row(a, _):
        for c in range(3):
            step(3 * a + c + LEAD)
            core_stage(3 * a + c)
            near_tap(a, c)
        return 0

    for grp in range(WINDOW):
        line_start(grp)
    for load in loads[:2]:
        load.wait()
    ms[g] = jnp.zeros((ms.shape[1], 128), jnp.float32)
    for x in range(raw_mask.shape[1]):
        value = raw_mask[:, x, :].astype(jnp.float32)
        ms[g, :, x * (span_y // B) : (x + 1) * (span_y // B)] = value
    flags = columns(ms, [(g, j) for j in range(n * deep // B)])
    for i in range(n):
        spread(flags, i)
    for k in range(n):
        d = (g + n // 2 + k) % n
        mask_features(d)
        if k == n // 2:
            xs[g] = stage[g]
        else:
            exchange(stage, xs, x_send, x_recv, d).start()
            toward(d).start()

    lax.fori_loop(0, LEAD, lead, 0)
    acc[...] = jnp.zeros_like(acc)
    for i in range(1, n):
        d = (g + i) % n
        arrival(xs, x_send, x_recv, d).wait_recv()
        arrival(ms, m_send, m_recv, d).wait_recv()
    flags = columns(ms, [(i, g * (deep // B) + j) for i in range(n) for j in range(deep // B)])
    for i in range(n):
        spread(flags, i)
    lax.fori_loop(0, n, take_slab, 0)
    lax.fori_loop(0, 3, near_row, 0)
    lax.fori_loop(0, n, turn, 0)
    for order in range(3):
        step(near_taps + order + LEAD)
        core_stage(near_taps + order)
        far_stage(order)
        if order == 1:
            for i in range(n // 2):
                give(jnp.where(low, n // 2, 0) + i)
    for i in range(1, n // 2):
        give(g // (n // 2) * (n // 2) + (g + i) % (n // 2))

    def deliver(d, source):
        for z in range(deep):
            raw[d * deep + z] = source[z * plane : (z + 1) * plane].reshape(raw.shape[1:])
        return pltpu.make_async_copy(raw.at[pl.ds(d * deep, deep)], out.at[pl.ds(d * deep, deep)], out_sem.at[d])

    deliver(g, total[slab(g)] * keep(slab(g))).start()
    lax.fori_loop(0, taps, finish_all, 0)
    for i in range(1, n):
        d = (g + i) % n
        toward(d).wait_send()
        exchange(stage, back, r_send, r_recv, d).wait_send()
    for k in list(range(n // 2 + 1, n)) + list(range(n // 2)):
        d = (g + n // 2 + k) % n
        arrival(back, r_send, r_recv, d).wait_recv()
        deliver(d, back[d]).start()
    for d in range(n):
        pltpu.make_async_copy(raw.at[pl.ds(d * deep, deep)], out.at[pl.ds(d * deep, deep)], out_sem.at[d]).wait()


def fits(features, weight):
    slab_z, slab_x, span_y, channels = features.shape
    n, m = lax.axis_size("gz"), lax.axis_size("xy")
    deep, plane, part = slab_z // n, span_y * slab_x, weight.shape[2]
    return (
        FAR_DILATION >= span_y > NEAR_DILATION
        and NEAR_DILATION >= slab_x * m
        and NEAR_DILATION % slab_z == 0 and FAR_DILATION % slab_z == 0 and NEAR_DILATION < n * slab_z and FAR_DILATION < n * slab_z
        and n % 4 == 0 and 2 * FAR_DILATION >= n * slab_z and m % 2 == 0 and m >= 4
        and slab_z % (B * n) == 0 and slab_x % B == 0 and span_y % B == 0 and slab_z // B % 8 == 0
        and plane <= 128 and plane % 8 == 0 and NEAR_DILATION * slab_x % 8 == 0
        and deep * plane % 16 == 0 and deep * (span_y - NEAR_DILATION) * slab_x % 16 == 0
        and channels % 128 == 0 and part % 16 == 0 and part * m == channels
    )


def fast(features, block_mask, near_kernel_weight, far_kernel_weight):
    slab_z, slab_x, span_y, channels = features.shape
    n, m = lax.axis_size("gz"), lax.axis_size("xy")
    part = near_kernel_weight.shape[2]
    deep, plane = slab_z // n, span_y * slab_x
    rows, side = deep * plane, deep * (span_y - NEAR_DILATION) * slab_x
    near = jnp.swapaxes(near_kernel_weight, 1, 2)
    far = jnp.swapaxes(far_kernel_weight, 1, 2)
    feat = jnp.swapaxes(features, 1, 2)
    taps = 12
    line = m // 2
    dma = pltpu.SemaphoreType.DMA
    hbm = pl.BlockSpec(memory_space=pl.ANY)
    out = pl.pallas_call(
        functools.partial(section_kernel, n, deep, span_y, NEAR_DILATION // slab_z, FAR_DILATION // slab_z),
        out_shape=jax.ShapeDtypeStruct(feat.shape, jnp.float32),
        in_specs=[hbm] * 4,
        out_specs=hbm,
        scratch_shapes=[
            pltpu.VMEM((taps, 2, 2, line, part // 2, channels), jnp.float32),
            pltpu.VMEM(feat.shape, jnp.float32),
            pltpu.VMEM(block_mask.shape, jnp.int32),
            pltpu.VMEM((n, rows, channels), jnp.float32),
            pltpu.VMEM((n, rows, channels), jnp.float32),
            pltpu.VMEM((n, rows, channels), jnp.float32),
            pltpu.VMEM((n, slab_z // B, 128), jnp.float32),
            pltpu.VMEM((n * rows, 128), jnp.float32),
            pltpu.VMEM((n * rows, 3 * channels), jnp.bfloat16),
            pltpu.VMEM((n * side, 3 * channels), jnp.bfloat16),
            pltpu.VMEM((n * side, 3 * channels), jnp.bfloat16),
            pltpu.VMEM(((n + 2 * (NEAR_DILATION // slab_z)) * rows, channels), jnp.float32),
            pltpu.VMEM((n * rows, 3 * channels), jnp.bfloat16),
            pltpu.VMEM((n * rows, channels), jnp.float32),
            dma((line, taps)), dma((taps,)), dma((taps,)),
            dma((line, taps)), dma((taps,)), dma((taps,)),
            dma((n,)), dma((n,)), dma((n,)), dma((n,)), dma((n,)), dma((n,)), dma((8,)), dma((n,)),
        ],
        compiler_params=pltpu.CompilerParams(
            collective_id=0, has_side_effects=True, vmem_limit_bytes=60 * 1024 * 1024),
        cost_estimate=pl.CostEstimate(flops=3 * 10**9, bytes_accessed=4 * 10**6, transcendentals=0),
    )(feat, block_mask, near, far)
    return jnp.swapaxes(out, 1, 2)


def local(features, block_mask, near_kernel_weight, far_kernel_weight):
    form = fast if fits(features, near_kernel_weight) else general
    return form(features, block_mask, near_kernel_weight, far_kernel_weight)


def solution(mesh):
    in_specs = (
        P("gz", "xy", None, None),
        P("gz", "xy", None),
        P(None, None, "xy"),
        P(None, None, "xy"),
    )
    out_specs = P("gz", "xy", None, None)
    return jax.shard_map(local, mesh=mesh, in_specs=in_specs, out_specs=out_specs, check_vma=False)
```

```python
import functools

import jax
import jax.numpy as jnp
from jax import lax
from jax.experimental import pallas as pl
from jax.experimental.pallas import tpu as pltpu
from jax.sharding import PartitionSpec as P

B = 2
NEAR_DILATION = 16
FAR_DILATION = 32
WINDOW = 4
LEAD = 9
MESH = pl.DeviceIdType.MESH


def offsets(dilation, extent):
    return (-1, 0, 1) if dilation < extent else (0,)


def from_behind(block, axis, distance):
    if distance == 0:
        return block
    devices = range(lax.axis_size(axis))
    route = [(i - distance, i) for i in devices if i - distance in devices]
    return lax.ppermute(block, axis, route)


def reach(field, dilation):
    slab_z, slab_x, span_y, _ = field.shape
    return (
        offsets(dilation, slab_z * lax.axis_size("gz")),
        offsets(dilation, slab_x * lax.axis_size("xy")),
        offsets(dilation, span_y),
    )


def gathered(weight, taps):
    cube = weight.reshape((3, 3, 3) + weight.shape[1:])
    for dim, tap in enumerate(taps):
        cube = cube if len(tap) == 3 else lax.slice_in_dim(cube, 1, 2, axis=dim)
    flat = cube.reshape((-1,) + weight.shape[1:])
    return lax.all_gather(flat, "xy", axis=2, tiled=True)


def dilated_result(field, weight, taps, dilation):
    slab_z, slab_x, span_y, channels = field.shape
    windows = []
    for a in taps[0]:
        over_z = from_behind(field, "gz", -a * dilation // slab_z)
        for b in taps[1]:
            over_x = from_behind(over_z, "xy", -b * dilation // slab_x)
            for c in taps[2]:
                if c == 0:
                    windows.append(over_x)
                elif c < 0:
                    part = over_x[:, :, : span_y - dilation]
                    windows.append(jnp.pad(part, ((0, 0), (0, 0), (dilation, 0), (0, 0))))
                else:
                    part = over_x[:, :, dilation:]
                    windows.append(jnp.pad(part, ((0, 0), (0, 0), (0, dilation), (0, 0))))
    columns = jnp.concatenate(windows, 3).reshape(slab_z * slab_x * span_y, -1)
    summed = jnp.dot(
        columns,
        weight.reshape(-1, weight.shape[2]),
        precision=lax.Precision.HIGH,
        preferred_element_type=jnp.float32,
    )
    return summed.reshape(slab_z, slab_x, span_y, weight.shape[2])


def general(features, block_mask, near_kernel_weight, far_kernel_weight):
    near_taps = reach(features, NEAR_DILATION)
    far_taps = reach(features, FAR_DILATION)
    active = jnp.repeat(jnp.repeat(jnp.repeat(block_mask, B, 0), B, 1), B, 2)
    active = active.astype(jnp.float32)[..., None]
    near_weight = gathered(near_kernel_weight, near_taps)
    far_weight = gathered(far_kernel_weight, far_taps)
    masked = active * features
    hidden = active * jnp.maximum(
        dilated_result(masked, near_weight, near_taps, NEAR_DILATION), 0.0
    )
    return active * (masked + dilated_result(hidden, far_weight, far_taps, FAR_DILATION))


def section_kernel(
    n, deep, span_y, near_step, far_step,
    feat, mask, near, far, out,
    wall, ready, raw, raw_mask, stage, xs, ms, mf, xc, xl, xh, acc, hc, total,
    line_send, pair_send, core_send, line_recv, pair_recv, core_recv,
    x_send, x_recv, m_send, m_recv, r_send, r_recv, load_sem, out_sem,
):
    taps, _, _, line, half, channels = wall.shape
    slab_x = raw.shape[2]
    rows = xs.shape[1]
    plane = rows // deep
    skip = plane * NEAR_DILATION // span_y
    edge = plane - skip
    side = deep * edge
    near_taps = 9

    g = lax.axis_index("gz")
    s = lax.axis_index("xy")
    pos, col = s // 2, s % 2
    core = g % 2
    twin = g + 1 - 2 * core
    mate = s + 1 - 2 * col

    loads = [(mask, raw_mask), (feat, raw)]
    rows_of = pl.ds(pl.multiple_of(core * half, half), half)
    for a in range(3):
        loads.append((near.at[pl.ds(9 * a + 3, 3), rows_of], wall.at[pl.ds(3 * a, 3), core, col, pos]))
    for a in range(3):
        loads.append((far.at[9 * a + 4, rows_of], wall.at[near_taps + a, core, col, pos]))
    loads = [pltpu.make_async_copy(a, b, load_sem.at[i]) for i, (a, b) in enumerate(loads)]
    for load in loads:
        load.start()

    barrier = pltpu.get_barrier_semaphore()
    for i in range(1, n):
        pl.semaphore_signal(barrier, inc=1, device_id={"gz": (g + i) % n}, device_id_type=MESH)
    pl.semaphore_signal(barrier, inc=1, device_id={"xy": mate}, device_id_type=MESH)

    for i in range(1, line):
        pl.semaphore_signal(barrier, inc=1, device_id={"xy": 2 * ((pos + i) % line) + col}, device_id_type=MESH)

    for load in loads[2:]:
        load.wait()
    pl.semaphore_wait(barrier, n + line - 1)

    def along(k, grp):
        ref = wall.at[tap_of(grp), core, col, pos]
        where = 2 * ((pos + k) % line) + col
        return pltpu.make_async_remote_copy(
            ref, ref, line_send.at[k, grp], line_recv.at[pos, grp], device_id={"xy": where}, device_id_type=MESH)

    def from_line(p, grp):
        ref = wall.at[tap_of(grp), core, col, p]
        return pltpu.make_async_remote_copy(
            ref, ref, line_send.at[0, grp], line_recv.at[p, grp], device_id={"xy": 2 * p + col}, device_id_type=MESH)

    def across(q, grp):
        ref = wall.at[tap_of(grp), core, q]
        return pltpu.make_async_remote_copy(
            ref, ref, pair_send.at[grp], pair_recv.at[grp], device_id={"xy": mate}, device_id_type=MESH)

    def to_twin(h, grp):
        ref = wall.at[tap_of(grp), h]
        return pltpu.make_async_remote_copy(
            ref, ref, core_send.at[grp], core_recv.at[grp], device_id={"gz": twin}, device_id_type=MESH)

    def line_start(grp):
        for k in range(1, line):
            along(k, grp).start()

    def line_stage(grp):
        for k in range(1, line):
            from_line((pos + k) % line, grp).wait_recv()
        across(col, grp).start()

    def pair_stage(grp):
        across(1 - col, grp).wait_recv()
        to_twin(core, grp).start()

    def core_stage(grp):
        to_twin(1 - core, grp).wait_recv()

    def finish(grp):
        for k in range(1, line):
            along(k, grp).wait_send()
        across(col, grp).wait_send()
        to_twin(core, grp).wait_send()

    low = g < n // 2

    def tap_of(grp):
        return jnp.where(low | (grp < near_taps), grp, near_taps + taps - 1 - grp)

    def exchange(src, dst, send, recv, d):
        return pltpu.make_async_remote_copy(
            src.at[d], dst.at[g], send.at[d], recv.at[g], device_id={"gz": d}, device_id_type=MESH)

    def toward(d):
        return pltpu.make_async_remote_copy(
            ms.at[g], ms.at[g], m_send.at[d], m_recv.at[g], device_id={"gz": d}, device_id_type=MESH)

    def arrival(dst, send, recv, d):
        return pltpu.make_async_remote_copy(
            dst.at[d], dst.at[d], send.at[d], recv.at[d], device_id={"gz": d}, device_id_type=MESH)

    def split(value, ref, start, count):
        high = value.astype(jnp.bfloat16)
        low = (value - high.astype(jnp.float32)).astype(jnp.bfloat16)
        at = pl.ds(pl.multiple_of(start, 16), count)
        ref[at, 0:channels] = high
        ref[at, channels : 2 * channels] = low
        ref[at, 2 * channels :] = high

    def prepare(grp):
        core_stage(grp)
        tap = tap_of(grp)
        value = jnp.concatenate([wall[tap, h, q, p] for p in range(line) for q in range(2) for h in range(2)], axis=0)
        value = jnp.transpose(value)
        high = value.astype(jnp.bfloat16)
        low = (value - high.astype(jnp.float32)).astype(jnp.bfloat16)
        ready[grp, 0:channels] = high
        ready[grp, channels : 2 * channels] = high
        ready[grp, 2 * channels :] = low

    def product(lhs, weight):
        return jnp.dot(lhs, weight, preferred_element_type=jnp.float32)

    def columns(ref, picks):
        chosen = [ref[slab, pl.ds(row, 1), :] for slab, row in picks]
        chosen.append(jnp.zeros((-len(picks) % 8 + 8, 128), jnp.float32))
        r = lax.broadcasted_iota(jnp.int32, (plane, 128), 0)
        k = lax.broadcasted_iota(jnp.int32, (plane, 128), 1)
        block = (r % slab_x) // B * (span_y // B) + r // slab_x // B
        spots, chosen = (block == k).astype(jnp.float32), jnp.concatenate(chosen, axis=0)
        return lax.dot_general(spots, chosen, (((1,), (1,)), ((), ())), preferred_element_type=jnp.float32)

    def spread(flags, i):
        for z in range(deep):
            at = i * (deep // B) + z // B
            column = flags[:, at : at + 1]
            mf[i * rows + z * plane : i * rows + (z + 1) * plane, :] = jnp.broadcast_to(column, (plane, 128))

    def keep(at):
        return jnp.concatenate([mf[at]] * (channels // 128), axis=1)

    def mask_features(d):
        for z in range(deep):
            value = raw[d * deep + z].reshape(plane, channels)
            at = pl.ds(pl.multiple_of(d * rows + z * plane, 8), plane)
            stage[d, z * plane : (z + 1) * plane] = value * keep(at)

    def slab(i):
        return pl.ds(pl.multiple_of(i * rows, rows), rows)

    def near_tap(a, c):
        weight = ready[3 * a + c]
        base = pl.multiple_of((2 - a) * near_step * rows, rows)
        if c == 1:
            at = pl.ds(base, n * rows)
            acc[at] += product(xc[...], weight)
            return
        source, offset = (xl, skip) if c == 0 else (xh, 0)
        result = product(source[...], weight)
        for i in range(n * deep):
            at = pl.ds(pl.multiple_of(base + i * plane + offset, 8), edge)
            acc[at] += result[i * edge : (i + 1) * edge]

    def give(d):
        exchange(stage, xs, x_send, x_recv, d).wait_send()
        stage[d] = total[slab(d)] * keep(slab(d))
        exchange(stage, out, r_send, r_recv, d).start()

    def far_stage(order):
        weight = ready[near_taps + order]
        if order == 1:
            total[...] += product(hc[...], weight)
            return
        count = (n - far_step) * rows
        front = low if order == 0 else jnp.logical_not(low)
        source = pl.multiple_of(jnp.where(front, 0, far_step * rows), rows)
        target = pl.multiple_of(jnp.where(front, far_step * rows, 0), rows)
        total[pl.ds(target, count)] += product(hc[pl.ds(source, count)], weight)

    def turn(i, _):
        at = slab(i)
        value = jnp.maximum(acc[pl.ds(pl.multiple_of((i + near_step) * rows, rows), rows)], 0.0) * keep(at)
        split(value, hc, i * rows, rows)
        total[at] = xs[i]
        return 0

    def take_slab(i, _):
        value = xs[i]
        split(value, xc, i * rows, rows)
        planes = [value[z * plane : (z + 1) * plane] for z in range(deep)]
        split(jnp.concatenate([one[:edge] for one in planes], axis=0), xl, i * side, side)
        split(jnp.concatenate([one[skip:] for one in planes], axis=0), xh, i * side, side)
        return 0

    def step(tau):
        @pl.when(tau < taps)
        def _():
            line_stage(tau)

        @pl.when(tau + WINDOW < taps)
        def _():
            line_start(tau + WINDOW)

        @pl.when((tau >= 1) & (tau <= taps))
        def _():
            pair_stage(tau - 1)

        @pl.when((tau >= 2) & (tau <= taps + 1))
        def _():
            prepare(tau - 2)

    def finish_all(grp, _):
        finish(grp)
        return 0

    def lead(tau, _):
        step(tau)
        return 0

    def near_row(a, _):
        for c in range(3):
            near_tap(a, c)
            step(3 * a + c + LEAD)
        return 0

    for grp in range(WINDOW):
        line_start(grp)
    for load in loads[:2]:
        load.wait()
    ms[g] = jnp.zeros((ms.shape[1], 128), jnp.float32)
    for x in range(raw_mask.shape[1]):
        value = raw_mask[:, x, :].astype(jnp.float32)
        ms[g, :, x * (span_y // B) : (x + 1) * (span_y // B)] = value
    flags = columns(ms, [(g, j) for j in range(n * deep // B)])
    for i in range(n):
        spread(flags, i)
    for k in range(n):
        d = (g + n // 2 + k) % n
        mask_features(d)
        if k == n // 2:
            xs[g] = stage[g]
        else:
            exchange(stage, xs, x_send, x_recv, d).start()
            toward(d).start()

    lax.fori_loop(0, LEAD, lead, 0)
    acc[...] = jnp.zeros_like(acc)
    for i in range(1, n):
        d = (g + i) % n
        arrival(xs, x_send, x_recv, d).wait_recv()
        arrival(ms, m_send, m_recv, d).wait_recv()
    flags = columns(ms, [(i, g * (deep // B) + j) for i in range(n) for j in range(deep // B)])
    for i in range(n):
        spread(flags, i)
    lax.fori_loop(0, n, take_slab, 0)
    lax.fori_loop(0, 3, near_row, 0)
    lax.fori_loop(0, n, turn, 0)
    for order in range(3):
        far_stage(order)
        if order == 1:
            for i in range(n // 2):
                give(jnp.where(low, n // 2, 0) + i)
    for i in range(1, n // 2):
        give(g // (n // 2) * (n // 2) + (g + i) % (n // 2))

    stage[g] = total[slab(g)] * keep(slab(g))
    own = pltpu.make_async_copy(stage.at[g], out.at[g], out_sem)
    own.start()
    lax.fori_loop(0, taps, finish_all, 0)
    for i in range(1, n):
        d = (g + i) % n
        toward(d).wait_send()
        exchange(stage, out, r_send, r_recv, d).wait_send()
        arrival(out, r_send, r_recv, d).wait_recv()
    own.wait()


def fits(features, weight):
    slab_z, slab_x, span_y, channels = features.shape
    n, m = lax.axis_size("gz"), lax.axis_size("xy")
    deep, plane, part = slab_z // n, span_y * slab_x, weight.shape[2]
    return (
        FAR_DILATION >= span_y > NEAR_DILATION
        and NEAR_DILATION >= slab_x * m
        and NEAR_DILATION % slab_z == 0 and FAR_DILATION % slab_z == 0 and NEAR_DILATION < n * slab_z and FAR_DILATION < n * slab_z
        and n % 4 == 0 and 2 * FAR_DILATION >= n * slab_z and m % 2 == 0 and m >= 4
        and slab_z % (B * n) == 0 and slab_x % B == 0 and span_y % B == 0 and slab_z // B % 8 == 0
        and plane <= 128 and plane % 8 == 0 and NEAR_DILATION * slab_x % 8 == 0
        and deep * plane % 16 == 0 and deep * (span_y - NEAR_DILATION) * slab_x % 16 == 0
        and channels % 128 == 0 and part % 16 == 0 and part * m == channels
    )


def fast(features, block_mask, near_kernel_weight, far_kernel_weight):
    slab_z, slab_x, span_y, channels = features.shape
    n, m = lax.axis_size("gz"), lax.axis_size("xy")
    part = near_kernel_weight.shape[2]
    deep, plane = slab_z // n, span_y * slab_x
    rows, side = deep * plane, deep * (span_y - NEAR_DILATION) * slab_x
    near = jnp.swapaxes(near_kernel_weight, 1, 2)
    far = jnp.swapaxes(far_kernel_weight, 1, 2)
    feat = jnp.swapaxes(features, 1, 2)
    taps = 12
    line = m // 2
    dma = pltpu.SemaphoreType.DMA
    out = pl.pallas_call(
        functools.partial(section_kernel, n, deep, span_y, NEAR_DILATION // slab_z, FAR_DILATION // slab_z),
        out_shape=jax.ShapeDtypeStruct((n, rows, channels), jnp.float32),
        in_specs=[pl.BlockSpec(memory_space=pltpu.HBM)] * 4,
        out_specs=pl.BlockSpec(memory_space=pl.ANY),
        scratch_shapes=[
            pltpu.VMEM((taps, 2, 2, line, part // 2, channels), jnp.float32),
            pltpu.VMEM((taps, 3 * channels, m * part), jnp.bfloat16),
            pltpu.VMEM(feat.shape, jnp.float32),
            pltpu.VMEM(block_mask.shape, jnp.int32),
            pltpu.VMEM((n, rows, channels), jnp.float32),
            pltpu.VMEM((n, rows, channels), jnp.float32),
            pltpu.VMEM((n, slab_z // B, 128), jnp.float32),
            pltpu.VMEM((n * rows, 128), jnp.float32),
            pltpu.VMEM((n * rows, 3 * channels), jnp.bfloat16),
            pltpu.VMEM((n * side, 3 * channels), jnp.bfloat16),
            pltpu.VMEM((n * side, 3 * channels), jnp.bfloat16),
            pltpu.VMEM(((n + 2 * (NEAR_DILATION // slab_z)) * rows, channels), jnp.float32),
            pltpu.VMEM((n * rows, 3 * channels), jnp.bfloat16),
            pltpu.VMEM((n * rows, channels), jnp.float32),
            dma((line, taps)), dma((taps,)), dma((taps,)),
            dma((line, taps)), dma((taps,)), dma((taps,)),
            dma((n,)), dma((n,)), dma((n,)), dma((n,)), dma((n,)), dma((n,)), dma((8,)), dma,
        ],
        compiler_params=pltpu.CompilerParams(
            collective_id=0, has_side_effects=True, vmem_limit_bytes=60 * 1024 * 1024),
        cost_estimate=pl.CostEstimate(flops=3 * 10**9, bytes_accessed=4 * 10**6, transcendentals=0),
    )(feat, block_mask, near, far)
    return jnp.swapaxes(out.reshape(feat.shape), 1, 2)


def local(features, block_mask, near_kernel_weight, far_kernel_weight):
    form = fast if fits(features, near_kernel_weight) else general
    return form(features, block_mask, near_kernel_weight, far_kernel_weight)


def solution(mesh):
    in_specs = (
        P("gz", "xy", None, None),
        P("gz", "xy", None),
        P(None, None, "xy"),
        P(None, None, "xy"),
    )
    out_specs = P("gz", "xy", None, None)
    return jax.shard_map(local, mesh=mesh, in_specs=in_specs, out_specs=out_specs, check_vma=False)
```

```python
import functools

import jax
import jax.numpy as jnp
from jax import lax
from jax.experimental import pallas as pl
from jax.experimental.pallas import tpu as pltpu
from jax.sharding import PartitionSpec as P

B = 2
NEAR_DILATION = 16
FAR_DILATION = 32
WINDOW = 4
LEAD = 9
LAG = 3
MESH = pl.DeviceIdType.MESH


def offsets(dilation, extent):
    return (-1, 0, 1) if dilation < extent else (0,)


def from_behind(block, axis, distance):
    if distance == 0:
        return block
    devices = range(lax.axis_size(axis))
    route = [(i - distance, i) for i in devices if i - distance in devices]
    return lax.ppermute(block, axis, route)


def reach(field, dilation):
    slab_z, slab_x, span_y, _ = field.shape
    return (
        offsets(dilation, slab_z * lax.axis_size("gz")),
        offsets(dilation, slab_x * lax.axis_size("xy")),
        offsets(dilation, span_y),
    )


def gathered(weight, taps):
    cube = weight.reshape((3, 3, 3) + weight.shape[1:])
    for dim, tap in enumerate(taps):
        cube = cube if len(tap) == 3 else lax.slice_in_dim(cube, 1, 2, axis=dim)
    flat = cube.reshape((-1,) + weight.shape[1:])
    return lax.all_gather(flat, "xy", axis=2, tiled=True)


def dilated_result(field, weight, taps, dilation):
    slab_z, slab_x, span_y, channels = field.shape
    windows = []
    for a in taps[0]:
        over_z = from_behind(field, "gz", -a * dilation // slab_z)
        for b in taps[1]:
            over_x = from_behind(over_z, "xy", -b * dilation // slab_x)
            for c in taps[2]:
                if c == 0:
                    windows.append(over_x)
                elif c < 0:
                    part = over_x[:, :, : span_y - dilation]
                    windows.append(jnp.pad(part, ((0, 0), (0, 0), (dilation, 0), (0, 0))))
                else:
                    part = over_x[:, :, dilation:]
                    windows.append(jnp.pad(part, ((0, 0), (0, 0), (0, dilation), (0, 0))))
    columns = jnp.concatenate(windows, 3).reshape(slab_z * slab_x * span_y, -1)
    summed = jnp.dot(
        columns,
        weight.reshape(-1, weight.shape[2]),
        precision=lax.Precision.HIGH,
        preferred_element_type=jnp.float32,
    )
    return summed.reshape(slab_z, slab_x, span_y, weight.shape[2])


def general(features, block_mask, near_kernel_weight, far_kernel_weight):
    near_taps = reach(features, NEAR_DILATION)
    far_taps = reach(features, FAR_DILATION)
    active = jnp.repeat(jnp.repeat(jnp.repeat(block_mask, B, 0), B, 1), B, 2)
    active = active.astype(jnp.float32)[..., None]
    near_weight = gathered(near_kernel_weight, near_taps)
    far_weight = gathered(far_kernel_weight, far_taps)
    masked = active * features
    hidden = active * jnp.maximum(
        dilated_result(masked, near_weight, near_taps, NEAR_DILATION), 0.0
    )
    return active * (masked + dilated_result(hidden, far_weight, far_taps, FAR_DILATION))


def section_kernel(
    n, deep, span_y, near_step, far_step,
    feat, mask, near, far, out,
    wall, ready, raw, raw_mask, stage, xs, ms, mf, xc, xl, xh, acc, hc, total,
    line_send, pair_send, core_send, line_recv, pair_recv, core_recv,
    x_send, x_recv, m_send, m_recv, r_send, r_recv, load_sem, out_sem,
):
    taps, _, _, line, half, channels = wall.shape
    slab_x = raw.shape[2]
    rows = xs.shape[1]
    plane = rows // deep
    skip = plane * NEAR_DILATION // span_y
    edge = plane - skip
    side = deep * edge
    near_taps = 9

    g = lax.axis_index("gz")
    s = lax.axis_index("xy")
    pos, col = s // 2, s % 2
    core = g % 2
    twin = g + 1 - 2 * core
    mate = s + 1 - 2 * col

    loads = [(mask, raw_mask), (feat, raw)]
    rows_of = pl.ds(pl.multiple_of(core * half, half), half)
    for a in range(3):
        loads.append((near.at[pl.ds(9 * a + 3, 3), rows_of], wall.at[pl.ds(3 * a, 3), core, col, pos]))
    for a in range(3):
        loads.append((far.at[9 * a + 4, rows_of], wall.at[near_taps + a, core, col, pos]))
    loads = [pltpu.make_async_copy(a, b, load_sem.at[i]) for i, (a, b) in enumerate(loads)]
    for load in loads:
        load.start()

    barrier = pltpu.get_barrier_semaphore()
    for i in range(1, n):
        pl.semaphore_signal(barrier, inc=1, device_id={"gz": (g + i) % n}, device_id_type=MESH)
    pl.semaphore_signal(barrier, inc=1, device_id={"xy": mate}, device_id_type=MESH)

    for i in range(1, line):
        pl.semaphore_signal(barrier, inc=1, device_id={"xy": 2 * ((pos + i) % line) + col}, device_id_type=MESH)

    for load in loads[2:]:
        load.wait()
    pl.semaphore_wait(barrier, n + line - 1)

    def along(k, grp):
        ref = wall.at[tap_of(grp), core, col, pos]
        where = 2 * ((pos + k) % line) + col
        return pltpu.make_async_remote_copy(
            ref, ref, line_send.at[k, grp], line_recv.at[pos, grp], device_id={"xy": where}, device_id_type=MESH)

    def from_line(p, grp):
        ref = wall.at[tap_of(grp), core, col, p]
        return pltpu.make_async_remote_copy(
            ref, ref, line_send.at[0, grp], line_recv.at[p, grp], device_id={"xy": 2 * p + col}, device_id_type=MESH)

    def across(q, grp):
        ref = wall.at[tap_of(grp), core, q]
        return pltpu.make_async_remote_copy(
            ref, ref, pair_send.at[grp], pair_recv.at[grp], device_id={"xy": mate}, device_id_type=MESH)

    def to_twin(h, grp):
        ref = wall.at[tap_of(grp), h]
        return pltpu.make_async_remote_copy(
            ref, ref, core_send.at[grp], core_recv.at[grp], device_id={"gz": twin}, device_id_type=MESH)

    def line_start(grp):
        for k in range(1, line):
            along(k, grp).start()

    def line_stage(grp):
        for k in range(1, line):
            from_line((pos + k) % line, grp).wait_recv()
        across(col, grp).start()

    def pair_stage(grp):
        across(1 - col, grp).wait_recv()
        to_twin(core, grp).start()

    def core_stage(grp):
        to_twin(1 - core, grp).wait_recv()

    def finish(grp):
        for k in range(1, line):
            along(k, grp).wait_send()
        across(col, grp).wait_send()
        to_twin(core, grp).wait_send()

    low = g < n // 2

    def tap_of(grp):
        return jnp.where(low | (grp < near_taps), grp, near_taps + taps - 1 - grp)

    def exchange(src, dst, send, recv, d):
        return pltpu.make_async_remote_copy(
            src.at[d], dst.at[g], send.at[d], recv.at[g], device_id={"gz": d}, device_id_type=MESH)

    def toward(d):
        return pltpu.make_async_remote_copy(
            ms.at[g], ms.at[g], m_send.at[d], m_recv.at[g], device_id={"gz": d}, device_id_type=MESH)

    def arrival(dst, send, recv, d):
        return pltpu.make_async_remote_copy(
            dst.at[d], dst.at[d], send.at[d], recv.at[d], device_id={"gz": d}, device_id_type=MESH)

    def split(value, ref, start, count):
        high = value.astype(jnp.bfloat16)
        low = (value - high.astype(jnp.float32)).astype(jnp.bfloat16)
        at = pl.ds(pl.multiple_of(start, 16), count)
        ref[at, 0:channels] = high
        ref[at, channels : 2 * channels] = low
        ref[at, 2 * channels :] = high

    def prepare(grp):
        core_stage(grp)
        tap = tap_of(grp)
        value = jnp.concatenate([wall[tap, h, q, p] for p in range(line) for q in range(2) for h in range(2)], axis=0)
        value = jnp.transpose(value)
        high = value.astype(jnp.bfloat16)
        low = (value - high.astype(jnp.float32)).astype(jnp.bfloat16)
        ready[grp, 0:channels] = high
        ready[grp, channels : 2 * channels] = high
        ready[grp, 2 * channels :] = low

    def product(lhs, weight):
        return jnp.dot(lhs, weight, preferred_element_type=jnp.float32)

    def columns(ref, picks):
        chosen = [ref[slab, pl.ds(row, 1), :] for slab, row in picks]
        chosen.append(jnp.zeros((-len(picks) % 8 + 8, 128), jnp.float32))
        r = lax.broadcasted_iota(jnp.int32, (plane, 128), 0)
        k = lax.broadcasted_iota(jnp.int32, (plane, 128), 1)
        block = (r % slab_x) // B * (span_y // B) + r // slab_x // B
        spots, chosen = (block == k).astype(jnp.float32), jnp.concatenate(chosen, axis=0)
        return lax.dot_general(spots, chosen, (((1,), (1,)), ((), ())), preferred_element_type=jnp.float32)

    def spread(flags, i):
        for z in range(deep):
            at = i * (deep // B) + z // B
            column = flags[:, at : at + 1]
            mf[i * rows + z * plane : i * rows + (z + 1) * plane, :] = jnp.broadcast_to(column, (plane, 128))

    def keep(at):
        return jnp.concatenate([mf[at]] * (channels // 128), axis=1)

    def mask_features(d):
        for z in range(deep):
            value = raw[d * deep + z].reshape(plane, channels)
            at = pl.ds(pl.multiple_of(d * rows + z * plane, 8), plane)
            stage[d, z * plane : (z + 1) * plane] = value * keep(at)

    def slab(i):
        return pl.ds(pl.multiple_of(i * rows, rows), rows)

    def near_tap(a, c):
        weight = ready[3 * a + c]
        base = pl.multiple_of((2 - a) * near_step * rows, rows)
        if c == 1:
            at = pl.ds(base, n * rows)
            acc[at] += product(xc[...], weight)
            return
        source, offset = (xl, skip) if c == 0 else (xh, 0)
        result = product(source[...], weight)
        for i in range(n * deep):
            at = pl.ds(pl.multiple_of(base + i * plane + offset, 8), edge)
            acc[at] += result[i * edge : (i + 1) * edge]

    def give(d):
        exchange(stage, xs, x_send, x_recv, d).wait_send()
        stage[d] = total[slab(d)] * keep(slab(d))
        exchange(stage, out, r_send, r_recv, d).start()

    def far_stage(order):
        weight = ready[near_taps + order]
        if order == 1:
            total[...] += product(hc[...], weight)
            return
        count = (n - far_step) * rows
        front = low if order == 0 else jnp.logical_not(low)
        source = pl.multiple_of(jnp.where(front, 0, far_step * rows), rows)
        target = pl.multiple_of(jnp.where(front, far_step * rows, 0), rows)
        total[pl.ds(target, count)] += product(hc[pl.ds(source, count)], weight)

    def turn(i, _):
        at = slab(i)
        value = jnp.maximum(acc[pl.ds(pl.multiple_of((i + near_step) * rows, rows), rows)], 0.0) * keep(at)
        split(value, hc, i * rows, rows)
        total[at] = xs[i]
        return 0

    def take_slab(i, _):
        value = xs[i]
        split(value, xc, i * rows, rows)
        planes = [value[z * plane : (z + 1) * plane] for z in range(deep)]
        split(jnp.concatenate([one[:edge] for one in planes], axis=0), xl, i * side, side)
        split(jnp.concatenate([one[skip:] for one in planes], axis=0), xh, i * side, side)
        return 0

    def step(tau):
        @pl.when(tau < taps)
        def _():
            line_stage(tau)

        @pl.when(tau + WINDOW < taps)
        def _():
            line_start(tau + WINDOW)

        @pl.when((tau >= LAG) & (tau < taps + LAG))
        def _():
            pair_stage(tau - LAG)

    def finish_all(grp, _):
        finish(grp)
        return 0

    def lead(tau, _):
        step(tau)

        @pl.when(tau >= 2 * LAG)
        def _():
            prepare(tau - 2 * LAG)

        return 0

    def near_row(a, _):
        for c in range(3):
            tap = 3 * a + c
            near_tap(a, c)
            step(tap + LEAD)

            @pl.when(tap + LEAD - 2 * LAG <= near_taps)
            def _():
                prepare(tap + LEAD - 2 * LAG)

        return 0

    for grp in range(WINDOW):
        line_start(grp)
    for load in loads[:2]:
        load.wait()
    ms[g] = jnp.zeros((ms.shape[1], 128), jnp.float32)
    for x in range(raw_mask.shape[1]):
        value = raw_mask[:, x, :].astype(jnp.float32)
        ms[g, :, x * (span_y // B) : (x + 1) * (span_y // B)] = value
    flags = columns(ms, [(g, j) for j in range(n * deep // B)])
    for i in range(n):
        spread(flags, i)
    for k in range(n):
        d = (g + n // 2 + k) % n
        mask_features(d)
        if k == n // 2:
            xs[g] = stage[g]
        else:
            exchange(stage, xs, x_send, x_recv, d).start()
            toward(d).start()

    lax.fori_loop(0, LEAD, lead, 0)
    acc[...] = jnp.zeros_like(acc)
    for i in range(1, n):
        d = (g + i) % n
        arrival(xs, x_send, x_recv, d).wait_recv()
        arrival(ms, m_send, m_recv, d).wait_recv()
    flags = columns(ms, [(i, g * (deep // B) + j) for i in range(n) for j in range(deep // B)])
    for i in range(n):
        spread(flags, i)
    lax.fori_loop(0, n, take_slab, 0)
    lax.fori_loop(0, 3, near_row, 0)
    lax.fori_loop(0, n, turn, 0)
    for order in range(3):
        far_stage(order)
        if order == 1:
            for i in range(n // 2):
                give(jnp.where(low, n // 2, 0) + i)
        if order < 2:
            prepare(near_taps + order + 1)
    for i in range(1, n // 2):
        give(g // (n // 2) * (n // 2) + (g + i) % (n // 2))

    stage[g] = total[slab(g)] * keep(slab(g))
    own = pltpu.make_async_copy(stage.at[g], out.at[g], out_sem)
    own.start()
    lax.fori_loop(0, taps, finish_all, 0)
    for i in range(1, n):
        d = (g + i) % n
        toward(d).wait_send()
        exchange(stage, out, r_send, r_recv, d).wait_send()
        arrival(out, r_send, r_recv, d).wait_recv()
    own.wait()


def fits(features, weight):
    slab_z, slab_x, span_y, channels = features.shape
    n, m = lax.axis_size("gz"), lax.axis_size("xy")
    deep, plane, part = slab_z // n, span_y * slab_x, weight.shape[2]
    return (
        FAR_DILATION >= span_y > NEAR_DILATION
        and NEAR_DILATION >= slab_x * m
        and NEAR_DILATION % slab_z == 0 and FAR_DILATION % slab_z == 0 and NEAR_DILATION < n * slab_z and FAR_DILATION < n * slab_z
        and n % 4 == 0 and 2 * FAR_DILATION >= n * slab_z and m % 2 == 0 and m >= 4
        and slab_z % (B * n) == 0 and slab_x % B == 0 and span_y % B == 0 and slab_z // B % 8 == 0
        and plane <= 128 and plane % 8 == 0 and NEAR_DILATION * slab_x % 8 == 0
        and deep * plane % 16 == 0 and deep * (span_y - NEAR_DILATION) * slab_x % 16 == 0
        and channels % 128 == 0 and part % 16 == 0 and part * m == channels
    )


def fast(features, block_mask, near_kernel_weight, far_kernel_weight):
    slab_z, slab_x, span_y, channels = features.shape
    n, m = lax.axis_size("gz"), lax.axis_size("xy")
    part = near_kernel_weight.shape[2]
    deep, plane = slab_z // n, span_y * slab_x
    rows, side = deep * plane, deep * (span_y - NEAR_DILATION) * slab_x
    near = jnp.swapaxes(near_kernel_weight, 1, 2)
    far = jnp.swapaxes(far_kernel_weight, 1, 2)
    feat = jnp.swapaxes(features, 1, 2)
    taps = 12
    line = m // 2
    dma = pltpu.SemaphoreType.DMA
    out = pl.pallas_call(
        functools.partial(section_kernel, n, deep, span_y, NEAR_DILATION // slab_z, FAR_DILATION // slab_z),
        out_shape=jax.ShapeDtypeStruct((n, rows, channels), jnp.float32),
        in_specs=[pl.BlockSpec(memory_space=pltpu.HBM)] * 4,
        out_specs=pl.BlockSpec(memory_space=pl.ANY),
        scratch_shapes=[
            pltpu.VMEM((taps, 2, 2, line, part // 2, channels), jnp.float32),
            pltpu.VMEM((taps, 3 * channels, m * part), jnp.bfloat16),
            pltpu.VMEM(feat.shape, jnp.float32),
            pltpu.VMEM(block_mask.shape, jnp.int32),
            pltpu.VMEM((n, rows, channels), jnp.float32),
            pltpu.VMEM((n, rows, channels), jnp.float32),
            pltpu.VMEM((n, slab_z // B, 128), jnp.float32),
            pltpu.VMEM((n * rows, 128), jnp.float32),
            pltpu.VMEM((n * rows, 3 * channels), jnp.bfloat16),
            pltpu.VMEM((n * side, 3 * channels), jnp.bfloat16),
            pltpu.VMEM((n * side, 3 * channels), jnp.bfloat16),
            pltpu.VMEM(((n + 2 * (NEAR_DILATION // slab_z)) * rows, channels), jnp.float32),
            pltpu.VMEM((n * rows, 3 * channels), jnp.bfloat16),
            pltpu.VMEM((n * rows, channels), jnp.float32),
            dma((line, taps)), dma((taps,)), dma((taps,)),
            dma((line, taps)), dma((taps,)), dma((taps,)),
            dma((n,)), dma((n,)), dma((n,)), dma((n,)), dma((n,)), dma((n,)), dma((8,)), dma,
        ],
        compiler_params=pltpu.CompilerParams(
            collective_id=0, has_side_effects=True, vmem_limit_bytes=60 * 1024 * 1024),
        cost_estimate=pl.CostEstimate(flops=3 * 10**9, bytes_accessed=4 * 10**6, transcendentals=0),
    )(feat, block_mask, near, far)
    return jnp.swapaxes(out.reshape(feat.shape), 1, 2)


def local(features, block_mask, near_kernel_weight, far_kernel_weight):
    form = fast if fits(features, near_kernel_weight) else general
    return form(features, block_mask, near_kernel_weight, far_kernel_weight)


def solution(mesh):
    in_specs = (
        P("gz", "xy", None, None),
        P("gz", "xy", None),
        P(None, None, "xy"),
        P(None, None, "xy"),
    )
    out_specs = P("gz", "xy", None, None)
    return jax.shard_map(local, mesh=mesh, in_specs=in_specs, out_specs=out_specs, check_vma=False)
```

```python
import functools

import jax
import jax.numpy as jnp
from jax import lax
from jax.experimental import pallas as pl
from jax.experimental.pallas import tpu as pltpu
from jax.sharding import PartitionSpec as P

B = 2
NEAR_DILATION = 16
FAR_DILATION = 32
WINDOW = 6
LEAD = 9
LAG = 3
MESH = pl.DeviceIdType.MESH


def offsets(dilation, extent):
    return (-1, 0, 1) if dilation < extent else (0,)


def from_behind(block, axis, distance):
    if distance == 0:
        return block
    devices = range(lax.axis_size(axis))
    route = [(i - distance, i) for i in devices if i - distance in devices]
    return lax.ppermute(block, axis, route)


def reach(field, dilation):
    slab_z, slab_x, span_y, _ = field.shape
    return (
        offsets(dilation, slab_z * lax.axis_size("gz")),
        offsets(dilation, slab_x * lax.axis_size("xy")),
        offsets(dilation, span_y),
    )


def gathered(weight, taps):
    cube = weight.reshape((3, 3, 3) + weight.shape[1:])
    for dim, tap in enumerate(taps):
        cube = cube if len(tap) == 3 else lax.slice_in_dim(cube, 1, 2, axis=dim)
    flat = cube.reshape((-1,) + weight.shape[1:])
    return lax.all_gather(flat, "xy", axis=2, tiled=True)


def dilated_result(field, weight, taps, dilation):
    slab_z, slab_x, span_y, channels = field.shape
    windows = []
    for a in taps[0]:
        over_z = from_behind(field, "gz", -a * dilation // slab_z)
        for b in taps[1]:
            over_x = from_behind(over_z, "xy", -b * dilation // slab_x)
            for c in taps[2]:
                if c == 0:
                    windows.append(over_x)
                elif c < 0:
                    part = over_x[:, :, : span_y - dilation]
                    windows.append(jnp.pad(part, ((0, 0), (0, 0), (dilation, 0), (0, 0))))
                else:
                    part = over_x[:, :, dilation:]
                    windows.append(jnp.pad(part, ((0, 0), (0, 0), (0, dilation), (0, 0))))
    columns = jnp.concatenate(windows, 3).reshape(slab_z * slab_x * span_y, -1)
    summed = jnp.dot(
        columns,
        weight.reshape(-1, weight.shape[2]),
        precision=lax.Precision.HIGH,
        preferred_element_type=jnp.float32,
    )
    return summed.reshape(slab_z, slab_x, span_y, weight.shape[2])


def general(features, block_mask, near_kernel_weight, far_kernel_weight):
    near_taps = reach(features, NEAR_DILATION)
    far_taps = reach(features, FAR_DILATION)
    active = jnp.repeat(jnp.repeat(jnp.repeat(block_mask, B, 0), B, 1), B, 2)
    active = active.astype(jnp.float32)[..., None]
    near_weight = gathered(near_kernel_weight, near_taps)
    far_weight = gathered(far_kernel_weight, far_taps)
    masked = active * features
    hidden = active * jnp.maximum(
        dilated_result(masked, near_weight, near_taps, NEAR_DILATION), 0.0
    )
    return active * (masked + dilated_result(hidden, far_weight, far_taps, FAR_DILATION))


def section_kernel(
    n, deep, span_y, near_step, far_step,
    feat, mask, near, far, out,
    wall, ready, raw, raw_mask, stage, xs, ms, mf, xc, xl, xh, acc, hc, total,
    line_send, pair_send, core_send, line_recv, pair_recv, core_recv,
    x_send, x_recv, m_send, m_recv, r_send, r_recv, load_sem, out_sem,
):
    taps, _, _, line, half, channels = wall.shape
    slab_x = raw.shape[2]
    rows = xs.shape[1]
    plane = rows // deep
    skip = plane * NEAR_DILATION // span_y
    edge = plane - skip
    side = deep * edge
    near_taps = 9

    g = lax.axis_index("gz")
    s = lax.axis_index("xy")
    pos, col = s // 2, s % 2
    core = g % 2
    twin = g + 1 - 2 * core
    mate = s + 1 - 2 * col

    loads = [(mask, raw_mask), (feat, raw)]
    rows_of = pl.ds(pl.multiple_of(core * half, half), half)
    for a in range(3):
        loads.append((near.at[pl.ds(9 * a + 3, 3), rows_of], wall.at[pl.ds(3 * a, 3), core, col, pos]))
    for a in range(3):
        loads.append((far.at[9 * a + 4, rows_of], wall.at[near_taps + a, core, col, pos]))
    loads = [pltpu.make_async_copy(a, b, load_sem.at[i]) for i, (a, b) in enumerate(loads)]
    for load in loads:
        load.start()

    barrier = pltpu.get_barrier_semaphore()
    for i in range(1, n):
        pl.semaphore_signal(barrier, inc=1, device_id={"gz": (g + i) % n}, device_id_type=MESH)
    pl.semaphore_signal(barrier, inc=1, device_id={"xy": mate}, device_id_type=MESH)

    for i in range(1, line):
        pl.semaphore_signal(barrier, inc=1, device_id={"xy": 2 * ((pos + i) % line) + col}, device_id_type=MESH)

    for load in loads[2:]:
        load.wait()
    pl.semaphore_wait(barrier, n + line - 1)

    def along(k, grp):
        ref = wall.at[tap_of(grp), core, col, pos]
        where = 2 * ((pos + k) % line) + col
        return pltpu.make_async_remote_copy(
            ref, ref, line_send.at[k, grp], line_recv.at[pos, grp], device_id={"xy": where}, device_id_type=MESH)

    def from_line(p, grp):
        ref = wall.at[tap_of(grp), core, col, p]
        return pltpu.make_async_remote_copy(
            ref, ref, line_send.at[0, grp], line_recv.at[p, grp], device_id={"xy": 2 * p + col}, device_id_type=MESH)

    def across(q, grp):
        ref = wall.at[tap_of(grp), core, q]
        return pltpu.make_async_remote_copy(
            ref, ref, pair_send.at[grp], pair_recv.at[grp], device_id={"xy": mate}, device_id_type=MESH)

    def to_twin(h, grp):
        ref = wall.at[tap_of(grp), h]
        return pltpu.make_async_remote_copy(
            ref, ref, core_send.at[grp], core_recv.at[grp], device_id={"gz": twin}, device_id_type=MESH)

    def line_start(grp):
        for k in range(1, line):
            along(k, grp).start()

    def line_stage(grp):
        for k in range(1, line):
            from_line((pos + k) % line, grp).wait_recv()
        across(col, grp).start()

    def pair_stage(grp):
        across(1 - col, grp).wait_recv()
        to_twin(core, grp).start()

    def core_stage(grp):
        to_twin(1 - core, grp).wait_recv()

    def finish(grp):
        for k in range(1, line):
            along(k, grp).wait_send()
        across(col, grp).wait_send()
        to_twin(core, grp).wait_send()

    low = g < n // 2

    def tap_of(grp):
        return jnp.where(low | (grp < near_taps), grp, near_taps + taps - 1 - grp)

    def exchange(src, dst, send, recv, d):
        return pltpu.make_async_remote_copy(
            src.at[d], dst.at[g], send.at[d], recv.at[g], device_id={"gz": d}, device_id_type=MESH)

    def toward(d):
        return pltpu.make_async_remote_copy(
            ms.at[g], ms.at[g], m_send.at[d], m_recv.at[g], device_id={"gz": d}, device_id_type=MESH)

    def arrival(dst, send, recv, d):
        return pltpu.make_async_remote_copy(
            dst.at[d], dst.at[d], send.at[d], recv.at[d], device_id={"gz": d}, device_id_type=MESH)

    def split(value, ref, start, count):
        high = value.astype(jnp.bfloat16)
        low = (value - high.astype(jnp.float32)).astype(jnp.bfloat16)
        at = pl.ds(pl.multiple_of(start, 16), count)
        ref[at, 0:channels] = high
        ref[at, channels : 2 * channels] = low
        ref[at, 2 * channels :] = high

    def prepare(grp):
        core_stage(grp)
        tap = tap_of(grp)
        value = jnp.concatenate([wall[tap, h, q, p] for p in range(line) for q in range(2) for h in range(2)], axis=0)
        value = jnp.transpose(value)
        high = value.astype(jnp.bfloat16)
        low = (value - high.astype(jnp.float32)).astype(jnp.bfloat16)
        ready[grp, 0:channels] = high
        ready[grp, channels : 2 * channels] = high
        ready[grp, 2 * channels :] = low

    def product(lhs, weight):
        return jnp.dot(lhs, weight, preferred_element_type=jnp.float32)

    def columns(ref, picks):
        chosen = [ref[slab, pl.ds(row, 1), :] for slab, row in picks]
        chosen.append(jnp.zeros((-len(picks) % 8 + 8, 128), jnp.float32))
        r = lax.broadcasted_iota(jnp.int32, (plane, 128), 0)
        k = lax.broadcasted_iota(jnp.int32, (plane, 128), 1)
        block = (r % slab_x) // B * (span_y // B) + r // slab_x // B
        spots, chosen = (block == k).astype(jnp.float32), jnp.concatenate(chosen, axis=0)
        return lax.dot_general(spots, chosen, (((1,), (1,)), ((), ())), preferred_element_type=jnp.float32)

    def spread(flags, i):
        for z in range(deep):
            at = i * (deep // B) + z // B
            column = flags[:, at : at + 1]
            mf[i * rows + z * plane : i * rows + (z + 1) * plane, :] = jnp.broadcast_to(column, (plane, 128))

    def keep(at):
        return jnp.concatenate([mf[at]] * (channels // 128), axis=1)

    def mask_features(d):
        for z in range(deep):
            value = raw[d * deep + z].reshape(plane, channels)
            at = pl.ds(pl.multiple_of(d * rows + z * plane, 8), plane)
            stage[d, z * plane : (z + 1) * plane] = value * keep(at)

    def slab(i):
        return pl.ds(pl.multiple_of(i * rows, rows), rows)

    def near_tap(a, c):
        weight = ready[3 * a + c]
        base = pl.multiple_of((2 - a) * near_step * rows, rows)
        if c == 1:
            at = pl.ds(base, n * rows)
            acc[at] += product(xc[...], weight)
            return
        source, offset = (xl, skip) if c == 0 else (xh, 0)
        result = product(source[...], weight)
        for i in range(n * deep):
            at = pl.ds(pl.multiple_of(base + i * plane + offset, 8), edge)
            acc[at] += result[i * edge : (i + 1) * edge]

    def give(d):
        exchange(stage, xs, x_send, x_recv, d).wait_send()
        stage[d] = total[slab(d)] * keep(slab(d))
        exchange(stage, out, r_send, r_recv, d).start()

    def far_stage(order):
        weight = ready[near_taps + order]
        if order == 1:
            total[...] += product(hc[...], weight)
            return
        count = (n - far_step) * rows
        front = low if order == 0 else jnp.logical_not(low)
        source = pl.multiple_of(jnp.where(front, 0, far_step * rows), rows)
        target = pl.multiple_of(jnp.where(front, far_step * rows, 0), rows)
        total[pl.ds(target, count)] += product(hc[pl.ds(source, count)], weight)

    def turn(i, _):
        at = slab(i)
        value = jnp.maximum(acc[pl.ds(pl.multiple_of((i + near_step) * rows, rows), rows)], 0.0) * keep(at)
        split(value, hc, i * rows, rows)
        total[at] = xs[i]
        return 0

    def take_slab(i, _):
        value = xs[i]
        split(value, xc, i * rows, rows)
        planes = [value[z * plane : (z + 1) * plane] for z in range(deep)]
        split(jnp.concatenate([one[:edge] for one in planes], axis=0), xl, i * side, side)
        split(jnp.concatenate([one[skip:] for one in planes], axis=0), xh, i * side, side)
        return 0

    def step(tau):
        @pl.when(tau < taps)
        def _():
            line_stage(tau)

        @pl.when(tau + WINDOW < taps)
        def _():
            line_start(tau + WINDOW)

        @pl.when((tau >= LAG) & (tau < taps + LAG))
        def _():
            pair_stage(tau - LAG)

    def finish_all(grp, _):
        finish(grp)
        return 0

    def lead(tau, _):
        step(tau)

        @pl.when(tau >= 2 * LAG)
        def _():
            prepare(tau - 2 * LAG)

        return 0

    def near_row(a, _):
        for c in range(3):
            tap = 3 * a + c
            near_tap(a, c)
            step(tap + LEAD)

            @pl.when(tap + LEAD - 2 * LAG <= near_taps)
            def _():
                prepare(tap + LEAD - 2 * LAG)

        return 0

    for grp in range(WINDOW):
        line_start(grp)
    for load in loads[:2]:
        load.wait()
    ms[g] = jnp.zeros((ms.shape[1], 128), jnp.float32)
    for x in range(raw_mask.shape[1]):
        value = raw_mask[:, x, :].astype(jnp.float32)
        ms[g, :, x * (span_y // B) : (x + 1) * (span_y // B)] = value
    flags = columns(ms, [(g, j) for j in range(n * deep // B)])
    for i in range(n):
        spread(flags, i)
    for k in range(n):
        d = (g + n // 2 + k) % n
        mask_features(d)
        if k == n // 2:
            xs[g] = stage[g]
        else:
            exchange(stage, xs, x_send, x_recv, d).start()
            toward(d).start()

    lax.fori_loop(0, LEAD, lead, 0)
    acc[...] = jnp.zeros_like(acc)
    for i in range(1, n):
        d = (g + i) % n
        arrival(xs, x_send, x_recv, d).wait_recv()
        arrival(ms, m_send, m_recv, d).wait_recv()
    flags = columns(ms, [(i, g * (deep // B) + j) for i in range(n) for j in range(deep // B)])
    for i in range(n):
        spread(flags, i)
    lax.fori_loop(0, n, take_slab, 0)
    lax.fori_loop(0, 3, near_row, 0)
    lax.fori_loop(0, n, turn, 0)
    for order in range(3):
        far_stage(order)
        if order == 1:
            for i in range(n // 2):
                give(jnp.where(low, n // 2, 0) + i)
        if order < 2:
            prepare(near_taps + order + 1)
    for i in range(1, n // 2):
        give(g // (n // 2) * (n // 2) + (g + i) % (n // 2))

    stage[g] = total[slab(g)] * keep(slab(g))
    own = pltpu.make_async_copy(stage.at[g], out.at[g], out_sem)
    own.start()
    lax.fori_loop(0, taps, finish_all, 0)
    for i in range(1, n):
        d = (g + i) % n
        toward(d).wait_send()
        exchange(stage, out, r_send, r_recv, d).wait_send()
        arrival(out, r_send, r_recv, d).wait_recv()
    own.wait()


def unfold_kernel(rows, cells):
    deep, span_y, slab_x, channels = cells.shape
    plane = span_y * slab_x
    for z in range(deep):
        cells[z] = rows[0, z * plane : (z + 1) * plane].reshape(span_y, slab_x, channels)


def fits(features, weight):
    slab_z, slab_x, span_y, channels = features.shape
    n, m = lax.axis_size("gz"), lax.axis_size("xy")
    deep, plane, part = slab_z // n, span_y * slab_x, weight.shape[2]
    return (
        FAR_DILATION >= span_y > NEAR_DILATION
        and NEAR_DILATION >= slab_x * m
        and NEAR_DILATION % slab_z == 0 and FAR_DILATION % slab_z == 0 and NEAR_DILATION < n * slab_z and FAR_DILATION < n * slab_z
        and n % 4 == 0 and 2 * FAR_DILATION >= n * slab_z and m % 2 == 0 and m >= 4
        and slab_z % (B * n) == 0 and slab_x % B == 0 and span_y % B == 0 and slab_z // B % 8 == 0
        and plane <= 128 and plane % 8 == 0 and NEAR_DILATION * slab_x % 8 == 0
        and deep * plane % 16 == 0 and deep * (span_y - NEAR_DILATION) * slab_x % 16 == 0
        and channels % 128 == 0 and part % 16 == 0 and part * m == channels
    )


def fast(features, block_mask, near_kernel_weight, far_kernel_weight):
    slab_z, slab_x, span_y, channels = features.shape
    n, m = lax.axis_size("gz"), lax.axis_size("xy")
    part = near_kernel_weight.shape[2]
    deep, plane = slab_z // n, span_y * slab_x
    rows, side = deep * plane, deep * (span_y - NEAR_DILATION) * slab_x
    near = jnp.swapaxes(near_kernel_weight, 1, 2)
    far = jnp.swapaxes(far_kernel_weight, 1, 2)
    feat = jnp.swapaxes(features, 1, 2)
    taps = 12
    line = m // 2
    dma = pltpu.SemaphoreType.DMA
    out = pl.pallas_call(
        functools.partial(section_kernel, n, deep, span_y, NEAR_DILATION // slab_z, FAR_DILATION // slab_z),
        out_shape=jax.ShapeDtypeStruct((n, rows, channels), jnp.float32),
        in_specs=[pl.BlockSpec(memory_space=pltpu.HBM)] * 4,
        out_specs=pl.BlockSpec(memory_space=pl.ANY),
        scratch_shapes=[
            pltpu.VMEM((taps, 2, 2, line, part // 2, channels), jnp.float32),
            pltpu.VMEM((taps, 3 * channels, m * part), jnp.bfloat16),
            pltpu.VMEM(feat.shape, jnp.float32),
            pltpu.VMEM(block_mask.shape, jnp.int32),
            pltpu.VMEM((n, rows, channels), jnp.float32),
            pltpu.VMEM((n, rows, channels), jnp.float32),
            pltpu.VMEM((n, slab_z // B, 128), jnp.float32),
            pltpu.VMEM((n * rows, 128), jnp.float32),
            pltpu.VMEM((n * rows, 3 * channels), jnp.bfloat16),
            pltpu.VMEM((n * side, 3 * channels), jnp.bfloat16),
            pltpu.VMEM((n * side, 3 * channels), jnp.bfloat16),
            pltpu.VMEM(((n + 2 * (NEAR_DILATION // slab_z)) * rows, channels), jnp.float32),
            pltpu.VMEM((n * rows, 3 * channels), jnp.bfloat16),
            pltpu.VMEM((n * rows, channels), jnp.float32),
            dma((line, taps)), dma((taps,)), dma((taps,)),
            dma((line, taps)), dma((taps,)), dma((taps,)),
            dma((n,)), dma((n,)), dma((n,)), dma((n,)), dma((n,)), dma((n,)), dma((8,)), dma,
        ],
        compiler_params=pltpu.CompilerParams(
            collective_id=0, has_side_effects=True, vmem_limit_bytes=60 * 1024 * 1024),
        cost_estimate=pl.CostEstimate(flops=3 * 10**9, bytes_accessed=4 * 10**6, transcendentals=0),
    )(feat, block_mask, near, far)
    cells = pl.pallas_call(
        unfold_kernel,
        out_shape=jax.ShapeDtypeStruct(feat.shape, jnp.float32),
        grid=(n,),
        in_specs=[pl.BlockSpec((1, rows, channels), lambda i: (i, 0, 0))],
        out_specs=pl.BlockSpec((deep, span_y, slab_x, channels), lambda i: (i, 0, 0, 0)),
    )(out)
    return jnp.swapaxes(cells, 1, 2)


def local(features, block_mask, near_kernel_weight, far_kernel_weight):
    form = fast if fits(features, near_kernel_weight) else general
    return form(features, block_mask, near_kernel_weight, far_kernel_weight)


def solution(mesh):
    in_specs = (
        P("gz", "xy", None, None),
        P("gz", "xy", None),
        P(None, None, "xy"),
        P(None, None, "xy"),
    )
    out_specs = P("gz", "xy", None, None)
    return jax.shard_map(local, mesh=mesh, in_specs=in_specs, out_specs=out_specs, check_vma=False)
```

```python
import functools

import jax
import jax.numpy as jnp
from jax import lax
from jax.experimental import pallas as pl
from jax.experimental.pallas import tpu as pltpu
from jax.sharding import PartitionSpec as P

B = 2
NEAR_DILATION = 16
FAR_DILATION = 32
WINDOW = 3
LEAD = 9
LAG = 3
MESH = pl.DeviceIdType.MESH


def offsets(dilation, extent):
    return (-1, 0, 1) if dilation < extent else (0,)


def from_behind(block, axis, distance):
    if distance == 0:
        return block
    devices = range(lax.axis_size(axis))
    route = [(i - distance, i) for i in devices if i - distance in devices]
    return lax.ppermute(block, axis, route)


def reach(field, dilation):
    slab_z, slab_x, span_y, _ = field.shape
    return (
        offsets(dilation, slab_z * lax.axis_size("gz")),
        offsets(dilation, slab_x * lax.axis_size("xy")),
        offsets(dilation, span_y),
    )


def gathered(weight, taps):
    cube = weight.reshape((3, 3, 3) + weight.shape[1:])
    for dim, tap in enumerate(taps):
        cube = cube if len(tap) == 3 else lax.slice_in_dim(cube, 1, 2, axis=dim)
    flat = cube.reshape((-1,) + weight.shape[1:])
    return lax.all_gather(flat, "xy", axis=2, tiled=True)


def dilated_result(field, weight, taps, dilation):
    slab_z, slab_x, span_y, channels = field.shape
    windows = []
    for a in taps[0]:
        over_z = from_behind(field, "gz", -a * dilation // slab_z)
        for b in taps[1]:
            over_x = from_behind(over_z, "xy", -b * dilation // slab_x)
            for c in taps[2]:
                if c == 0:
                    windows.append(over_x)
                elif c < 0:
                    part = over_x[:, :, : span_y - dilation]
                    windows.append(jnp.pad(part, ((0, 0), (0, 0), (dilation, 0), (0, 0))))
                else:
                    part = over_x[:, :, dilation:]
                    windows.append(jnp.pad(part, ((0, 0), (0, 0), (0, dilation), (0, 0))))
    columns = jnp.concatenate(windows, 3).reshape(slab_z * slab_x * span_y, -1)
    summed = jnp.dot(
        columns,
        weight.reshape(-1, weight.shape[2]),
        precision=lax.Precision.HIGH,
        preferred_element_type=jnp.float32,
    )
    return summed.reshape(slab_z, slab_x, span_y, weight.shape[2])


def general(features, block_mask, near_kernel_weight, far_kernel_weight):
    near_taps = reach(features, NEAR_DILATION)
    far_taps = reach(features, FAR_DILATION)
    active = jnp.repeat(jnp.repeat(jnp.repeat(block_mask, B, 0), B, 1), B, 2)
    active = active.astype(jnp.float32)[..., None]
    near_weight = gathered(near_kernel_weight, near_taps)
    far_weight = gathered(far_kernel_weight, far_taps)
    masked = active * features
    hidden = active * jnp.maximum(
        dilated_result(masked, near_weight, near_taps, NEAR_DILATION), 0.0
    )
    return active * (masked + dilated_result(hidden, far_weight, far_taps, FAR_DILATION))


def section_kernel(
    n, deep, span_y, near_step, far_step,
    feat, mask, near, far, out,
    wall, ready, raw, raw_mask, stage, xs, ms, mf, xc, xl, xh, acc, hc, total,
    line_send, pair_send, core_send, line_recv, pair_recv, core_recv,
    x_send, x_recv, m_send, m_recv, r_send, r_recv, load_sem, out_sem,
):
    taps, _, _, line, half, channels = wall.shape
    slab_x = raw.shape[2]
    rows = xs.shape[1]
    plane = rows // deep
    skip = plane * NEAR_DILATION // span_y
    edge = plane - skip
    side = deep * edge
    near_taps = 9

    g = lax.axis_index("gz")
    s = lax.axis_index("xy")
    pos, col = s // 2, s % 2
    core = g % 2
    twin = g + 1 - 2 * core
    mate = s + 1 - 2 * col

    loads = [(mask, raw_mask), (feat, raw)]
    rows_of = pl.ds(pl.multiple_of(core * half, half), half)
    for a in range(3):
        loads.append((near.at[pl.ds(9 * a + 3, 3), rows_of], wall.at[pl.ds(3 * a, 3), core, col, pos]))
    for a in range(3):
        loads.append((far.at[9 * a + 4, rows_of], wall.at[near_taps + a, core, col, pos]))
    loads = [pltpu.make_async_copy(a, b, load_sem.at[i]) for i, (a, b) in enumerate(loads)]
    for load in loads:
        load.start()

    barrier = pltpu.get_barrier_semaphore()
    for i in range(1, n):
        pl.semaphore_signal(barrier, inc=1, device_id={"gz": (g + i) % n}, device_id_type=MESH)
    pl.semaphore_signal(barrier, inc=1, device_id={"xy": mate}, device_id_type=MESH)

    for i in range(1, line):
        pl.semaphore_signal(barrier, inc=1, device_id={"xy": 2 * ((pos + i) % line) + col}, device_id_type=MESH)

    for load in loads[2:]:
        load.wait()
    pl.semaphore_wait(barrier, n + line - 1)

    def along(k, grp):
        ref = wall.at[tap_of(grp), core, col, pos]
        where = 2 * ((pos + k) % line) + col
        return pltpu.make_async_remote_copy(
            ref, ref, line_send.at[k, grp], line_recv.at[pos, grp], device_id={"xy": where}, device_id_type=MESH)

    def from_line(p, grp):
        ref = wall.at[tap_of(grp), core, col, p]
        return pltpu.make_async_remote_copy(
            ref, ref, line_send.at[0, grp], line_recv.at[p, grp], device_id={"xy": 2 * p + col}, device_id_type=MESH)

    def across(q, grp):
        ref = wall.at[tap_of(grp), core, q]
        return pltpu.make_async_remote_copy(
            ref, ref, pair_send.at[grp], pair_recv.at[grp], device_id={"xy": mate}, device_id_type=MESH)

    def to_twin(h, grp):
        ref = wall.at[tap_of(grp), h]
        return pltpu.make_async_remote_copy(
            ref, ref, core_send.at[grp], core_recv.at[grp], device_id={"gz": twin}, device_id_type=MESH)

    def line_start(grp):
        for k in range(1, line):
            along(k, grp).start()

    def line_stage(grp):
        for k in range(1, line):
            from_line((pos + k) % line, grp).wait_recv()
        across(col, grp).start()

    def pair_stage(grp):
        across(1 - col, grp).wait_recv()
        to_twin(core, grp).start()

    def core_stage(grp):
        to_twin(1 - core, grp).wait_recv()

    def finish(grp):
        for k in range(1, line):
            along(k, grp).wait_send()
        across(col, grp).wait_send()
        to_twin(core, grp).wait_send()

    low = g < n // 2

    def tap_of(grp):
        return jnp.where(low | (grp < near_taps), grp, near_taps + taps - 1 - grp)

    def exchange(src, dst, send, recv, d):
        return pltpu.make_async_remote_copy(
            src.at[d], dst.at[g], send.at[d], recv.at[g], device_id={"gz": d}, device_id_type=MESH)

    def toward(d):
        return pltpu.make_async_remote_copy(
            ms.at[g], ms.at[g], m_send.at[d], m_recv.at[g], device_id={"gz": d}, device_id_type=MESH)

    def arrival(dst, send, recv, d):
        return pltpu.make_async_remote_copy(
            dst.at[d], dst.at[d], send.at[d], recv.at[d], device_id={"gz": d}, device_id_type=MESH)

    def split(value, ref, start, count):
        high = value.astype(jnp.bfloat16)
        low = (value - high.astype(jnp.float32)).astype(jnp.bfloat16)
        at = pl.ds(pl.multiple_of(start, 16), count)
        ref[at, 0:channels] = high
        ref[at, channels : 2 * channels] = low
        ref[at, 2 * channels :] = high

    def prepare(grp):
        core_stage(grp)
        tap = tap_of(grp)
        value = jnp.concatenate([wall[tap, h, q, p] for p in range(line) for q in range(2) for h in range(2)], axis=0)
        value = jnp.transpose(value)
        high = value.astype(jnp.bfloat16)
        low = (value - high.astype(jnp.float32)).astype(jnp.bfloat16)
        ready[grp, 0:channels] = high
        ready[grp, channels : 2 * channels] = high
        ready[grp, 2 * channels :] = low

    def product(lhs, weight):
        return jnp.dot(lhs, weight, preferred_element_type=jnp.float32)

    def columns(ref, picks):
        chosen = [ref[slab, pl.ds(row, 1), :] for slab, row in picks]
        chosen.append(jnp.zeros((-len(picks) % 8 + 8, 128), jnp.float32))
        r = lax.broadcasted_iota(jnp.int32, (plane, 128), 0)
        k = lax.broadcasted_iota(jnp.int32, (plane, 128), 1)
        block = (r % slab_x) // B * (span_y // B) + r // slab_x // B
        spots, chosen = (block == k).astype(jnp.float32), jnp.concatenate(chosen, axis=0)
        return lax.dot_general(spots, chosen, (((1,), (1,)), ((), ())), preferred_element_type=jnp.float32)

    def spread(flags, i):
        for z in range(deep):
            at = i * (deep // B) + z // B
            column = flags[:, at : at + 1]
            mf[i * rows + z * plane : i * rows + (z + 1) * plane, :] = jnp.broadcast_to(column, (plane, 128))

    def keep(at):
        return jnp.concatenate([mf[at]] * (channels // 128), axis=1)

    def mask_features(d):
        for z in range(deep):
            value = raw[d * deep + z].reshape(plane, channels)
            at = pl.ds(pl.multiple_of(d * rows + z * plane, 8), plane)
            stage[d, z * plane : (z + 1) * plane] = value * keep(at)

    def slab(i):
        return pl.ds(pl.multiple_of(i * rows, rows), rows)

    def near_tap(a, c):
        weight = ready[3 * a + c]
        base = pl.multiple_of((2 - a) * near_step * rows, rows)
        if c == 1:
            at = pl.ds(base, n * rows)
            acc[at] += product(xc[...], weight)
            return
        source, offset = (xl, skip) if c == 0 else (xh, 0)
        result = product(source[...], weight)
        for i in range(n * deep):
            at = pl.ds(pl.multiple_of(base + i * plane + offset, 8), edge)
            acc[at] += result[i * edge : (i + 1) * edge]

    def give(d):
        exchange(stage, xs, x_send, x_recv, d).wait_send()
        stage[d] = total[slab(d)] * keep(slab(d))
        exchange(stage, out, r_send, r_recv, d).start()

    def far_stage(order):
        weight = ready[near_taps + order]
        if order == 1:
            total[...] += product(hc[...], weight)
            return
        count = (n - far_step) * rows
        front = low if order == 0 else jnp.logical_not(low)
        source = pl.multiple_of(jnp.where(front, 0, far_step * rows), rows)
        target = pl.multiple_of(jnp.where(front, far_step * rows, 0), rows)
        total[pl.ds(target, count)] += product(hc[pl.ds(source, count)], weight)

    def turn(i, _):
        at = slab(i)
        value = jnp.maximum(acc[pl.ds(pl.multiple_of((i + near_step) * rows, rows), rows)], 0.0) * keep(at)
        split(value, hc, i * rows, rows)
        total[at] = xs[i]
        return 0

    def take_slab(i, _):
        value = xs[i]
        split(value, xc, i * rows, rows)
        planes = [value[z * plane : (z + 1) * plane] for z in range(deep)]
        split(jnp.concatenate([one[:edge] for one in planes], axis=0), xl, i * side, side)
        split(jnp.concatenate([one[skip:] for one in planes], axis=0), xh, i * side, side)
        return 0

    def step(tau):
        @pl.when(tau < taps)
        def _():
            line_stage(tau)

        @pl.when(tau + WINDOW < taps)
        def _():
            line_start(tau + WINDOW)

        @pl.when((tau >= LAG) & (tau < taps + LAG))
        def _():
            pair_stage(tau - LAG)

    def finish_all(grp, _):
        finish(grp)
        return 0

    def lead(tau, _):
        step(tau)

        @pl.when(tau >= 2 * LAG)
        def _():
            prepare(tau - 2 * LAG)

        return 0

    def near_row(a, _):
        for c in range(3):
            tap = 3 * a + c
            near_tap(a, c)
            step(tap + LEAD)

            @pl.when(tap + LEAD - 2 * LAG <= near_taps)
            def _():
                prepare(tap + LEAD - 2 * LAG)

        return 0

    for grp in range(WINDOW):
        line_start(grp)
    for load in loads[:2]:
        load.wait()
    ms[g] = jnp.zeros((ms.shape[1], 128), jnp.float32)
    for x in range(raw_mask.shape[1]):
        value = raw_mask[:, x, :].astype(jnp.float32)
        ms[g, :, x * (span_y // B) : (x + 1) * (span_y // B)] = value
    flags = columns(ms, [(g, j) for j in range(n * deep // B)])
    for i in range(n):
        spread(flags, i)
    for k in range(n):
        d = (g + n // 2 + k) % n
        mask_features(d)
        if k == n // 2:
            xs[g] = stage[g]
        else:
            exchange(stage, xs, x_send, x_recv, d).start()
            toward(d).start()

    lax.fori_loop(0, LEAD, lead, 0)
    acc[...] = jnp.zeros_like(acc)
    for i in range(1, n):
        d = (g + i) % n
        arrival(xs, x_send, x_recv, d).wait_recv()
        arrival(ms, m_send, m_recv, d).wait_recv()
    flags = columns(ms, [(i, g * (deep // B) + j) for i in range(n) for j in range(deep // B)])
    for i in range(n):
        spread(flags, i)
    lax.fori_loop(0, n, take_slab, 0)
    lax.fori_loop(0, 3, near_row, 0)
    lax.fori_loop(0, n, turn, 0)
    for order in range(3):
        far_stage(order)
        if order == 1:
            for i in range(n // 2):
                give(jnp.where(low, n // 2, 0) + i)
        if order < 2:
            prepare(near_taps + order + 1)
    for i in range(1, n // 2):
        give(g // (n // 2) * (n // 2) + (g + i) % (n // 2))

    stage[g] = total[slab(g)] * keep(slab(g))
    own = pltpu.make_async_copy(stage.at[g], out.at[g], out_sem)
    own.start()
    lax.fori_loop(0, taps, finish_all, 0)
    for i in range(1, n):
        d = (g + i) % n
        toward(d).wait_send()
        exchange(stage, out, r_send, r_recv, d).wait_send()
        arrival(out, r_send, r_recv, d).wait_recv()
    own.wait()


def fits(features, weight):
    slab_z, slab_x, span_y, channels = features.shape
    n, m = lax.axis_size("gz"), lax.axis_size("xy")
    deep, plane, part = slab_z // n, span_y * slab_x, weight.shape[2]
    return (
        FAR_DILATION >= span_y > NEAR_DILATION
        and NEAR_DILATION >= slab_x * m
        and NEAR_DILATION % slab_z == 0 and FAR_DILATION % slab_z == 0 and NEAR_DILATION < n * slab_z and FAR_DILATION < n * slab_z
        and n % 4 == 0 and 2 * FAR_DILATION >= n * slab_z and m % 2 == 0 and m >= 4
        and slab_z % (B * n) == 0 and slab_x % B == 0 and span_y % B == 0 and slab_z // B % 8 == 0
        and plane <= 128 and plane % 8 == 0 and NEAR_DILATION * slab_x % 8 == 0
        and deep * plane % 16 == 0 and deep * (span_y - NEAR_DILATION) * slab_x % 16 == 0
        and channels % 128 == 0 and part % 16 == 0 and part * m == channels
    )


def fast(features, block_mask, near_kernel_weight, far_kernel_weight):
    slab_z, slab_x, span_y, channels = features.shape
    n, m = lax.axis_size("gz"), lax.axis_size("xy")
    part = near_kernel_weight.shape[2]
    deep, plane = slab_z // n, span_y * slab_x
    rows, side = deep * plane, deep * (span_y - NEAR_DILATION) * slab_x
    near = jnp.swapaxes(near_kernel_weight, 1, 2)
    far = jnp.swapaxes(far_kernel_weight, 1, 2)
    feat = jnp.swapaxes(features, 1, 2)
    taps = 12
    line = m // 2
    dma = pltpu.SemaphoreType.DMA
    out = pl.pallas_call(
        functools.partial(section_kernel, n, deep, span_y, NEAR_DILATION // slab_z, FAR_DILATION // slab_z),
        out_shape=jax.ShapeDtypeStruct((n, rows, channels), jnp.float32),
        in_specs=[pl.BlockSpec(memory_space=pltpu.HBM)] * 4,
        out_specs=pl.BlockSpec(memory_space=pl.ANY),
        scratch_shapes=[
            pltpu.VMEM((taps, 2, 2, line, part // 2, channels), jnp.float32),
            pltpu.VMEM((taps, 3 * channels, m * part), jnp.bfloat16),
            pltpu.VMEM(feat.shape, jnp.float32),
            pltpu.VMEM(block_mask.shape, jnp.int32),
            pltpu.VMEM((n, rows, channels), jnp.float32),
            pltpu.VMEM((n, rows, channels), jnp.float32),
            pltpu.VMEM((n, slab_z // B, 128), jnp.float32),
            pltpu.VMEM((n * rows, 128), jnp.float32),
            pltpu.VMEM((n * rows, 3 * channels), jnp.bfloat16),
            pltpu.VMEM((n * side, 3 * channels), jnp.bfloat16),
            pltpu.VMEM((n * side, 3 * channels), jnp.bfloat16),
            pltpu.VMEM(((n + 2 * (NEAR_DILATION // slab_z)) * rows, channels), jnp.float32),
            pltpu.VMEM((n * rows, 3 * channels), jnp.bfloat16),
            pltpu.VMEM((n * rows, channels), jnp.float32),
            dma((line, taps)), dma((taps,)), dma((taps,)),
            dma((line, taps)), dma((taps,)), dma((taps,)),
            dma((n,)), dma((n,)), dma((n,)), dma((n,)), dma((n,)), dma((n,)), dma((8,)), dma,
        ],
        compiler_params=pltpu.CompilerParams(
            collective_id=0, has_side_effects=True, vmem_limit_bytes=60 * 1024 * 1024),
        cost_estimate=pl.CostEstimate(flops=3 * 10**9, bytes_accessed=4 * 10**6, transcendentals=0),
    )(feat, block_mask, near, far)
    return jnp.swapaxes(out.reshape(feat.shape), 1, 2)


def local(features, block_mask, near_kernel_weight, far_kernel_weight):
    form = fast if fits(features, near_kernel_weight) else general
    return form(features, block_mask, near_kernel_weight, far_kernel_weight)


def solution(mesh):
    in_specs = (
        P("gz", "xy", None, None),
        P("gz", "xy", None),
        P(None, None, "xy"),
        P(None, None, "xy"),
    )
    out_specs = P("gz", "xy", None, None)
    return jax.shard_map(local, mesh=mesh, in_specs=in_specs, out_specs=out_specs, check_vma=False)
```

```python
import functools

import jax
import jax.numpy as jnp
from jax import lax
from jax.experimental import pallas as pl
from jax.experimental.pallas import tpu as pltpu
from jax.sharding import PartitionSpec as P

B = 2
NEAR_DILATION = 16
FAR_DILATION = 32
WINDOW = 3
LEAD = 9
LAG = 4
MESH = pl.DeviceIdType.MESH


def offsets(dilation, extent):
    return (-1, 0, 1) if dilation < extent else (0,)


def from_behind(block, axis, distance):
    if distance == 0:
        return block
    devices = range(lax.axis_size(axis))
    route = [(i - distance, i) for i in devices if i - distance in devices]
    return lax.ppermute(block, axis, route)


def reach(field, dilation):
    slab_z, slab_x, span_y, _ = field.shape
    return (
        offsets(dilation, slab_z * lax.axis_size("gz")),
        offsets(dilation, slab_x * lax.axis_size("xy")),
        offsets(dilation, span_y),
    )


def gathered(weight, taps):
    cube = weight.reshape((3, 3, 3) + weight.shape[1:])
    for dim, tap in enumerate(taps):
        cube = cube if len(tap) == 3 else lax.slice_in_dim(cube, 1, 2, axis=dim)
    flat = cube.reshape((-1,) + weight.shape[1:])
    return lax.all_gather(flat, "xy", axis=2, tiled=True)


def dilated_result(field, weight, taps, dilation):
    slab_z, slab_x, span_y, channels = field.shape
    windows = []
    for a in taps[0]:
        over_z = from_behind(field, "gz", -a * dilation // slab_z)
        for b in taps[1]:
            over_x = from_behind(over_z, "xy", -b * dilation // slab_x)
            for c in taps[2]:
                if c == 0:
                    windows.append(over_x)
                elif c < 0:
                    part = over_x[:, :, : span_y - dilation]
                    windows.append(jnp.pad(part, ((0, 0), (0, 0), (dilation, 0), (0, 0))))
                else:
                    part = over_x[:, :, dilation:]
                    windows.append(jnp.pad(part, ((0, 0), (0, 0), (0, dilation), (0, 0))))
    columns = jnp.concatenate(windows, 3).reshape(slab_z * slab_x * span_y, -1)
    summed = jnp.dot(
        columns,
        weight.reshape(-1, weight.shape[2]),
        precision=lax.Precision.HIGH,
        preferred_element_type=jnp.float32,
    )
    return summed.reshape(slab_z, slab_x, span_y, weight.shape[2])


def general(features, block_mask, near_kernel_weight, far_kernel_weight):
    near_taps = reach(features, NEAR_DILATION)
    far_taps = reach(features, FAR_DILATION)
    active = jnp.repeat(jnp.repeat(jnp.repeat(block_mask, B, 0), B, 1), B, 2)
    active = active.astype(jnp.float32)[..., None]
    near_weight = gathered(near_kernel_weight, near_taps)
    far_weight = gathered(far_kernel_weight, far_taps)
    masked = active * features
    hidden = active * jnp.maximum(
        dilated_result(masked, near_weight, near_taps, NEAR_DILATION), 0.0
    )
    return active * (masked + dilated_result(hidden, far_weight, far_taps, FAR_DILATION))


def section_kernel(
    n, deep, span_y, near_step, far_step,
    feat, mask, near, far, out,
    wall, ready, raw, raw_mask, stage, xs, ms, mf, xc, xl, xh, acc, hc, total,
    line_send, pair_send, core_send, line_recv, pair_recv, core_recv,
    x_send, x_recv, m_send, m_recv, r_send, r_recv, load_sem, out_sem,
):
    taps, _, _, line, half, channels = wall.shape
    slab_x = raw.shape[2]
    rows = xs.shape[1]
    plane = rows // deep
    skip = plane * NEAR_DILATION // span_y
    edge = plane - skip
    side = deep * edge
    near_taps = 9

    g = lax.axis_index("gz")
    s = lax.axis_index("xy")
    pos, col = s // 2, s % 2
    core = g % 2
    twin = g + 1 - 2 * core
    mate = s + 1 - 2 * col

    loads = [(mask, raw_mask), (feat, raw)]
    rows_of = pl.ds(pl.multiple_of(core * half, half), half)
    for a in range(3):
        loads.append((near.at[pl.ds(9 * a + 3, 3), rows_of], wall.at[pl.ds(3 * a, 3), core, col, pos]))
    for a in range(3):
        loads.append((far.at[9 * a + 4, rows_of], wall.at[near_taps + a, core, col, pos]))
    loads = [pltpu.make_async_copy(a, b, load_sem.at[i]) for i, (a, b) in enumerate(loads)]
    for load in loads:
        load.start()

    barrier = pltpu.get_barrier_semaphore()
    for i in range(1, n):
        pl.semaphore_signal(barrier, inc=1, device_id={"gz": (g + i) % n}, device_id_type=MESH)
    pl.semaphore_signal(barrier, inc=1, device_id={"xy": mate}, device_id_type=MESH)

    for i in range(1, line):
        pl.semaphore_signal(barrier, inc=1, device_id={"xy": 2 * ((pos + i) % line) + col}, device_id_type=MESH)

    for load in loads[2:]:
        load.wait()
    pl.semaphore_wait(barrier, n + line - 1)

    def along(k, grp):
        ref = wall.at[tap_of(grp), core, col, pos]
        where = 2 * ((pos + k) % line) + col
        return pltpu.make_async_remote_copy(
            ref, ref, line_send.at[k, grp], line_recv.at[pos, grp], device_id={"xy": where}, device_id_type=MESH)

    def from_line(p, grp):
        ref = wall.at[tap_of(grp), core, col, p]
        return pltpu.make_async_remote_copy(
            ref, ref, line_send.at[0, grp], line_recv.at[p, grp], device_id={"xy": 2 * p + col}, device_id_type=MESH)

    def across(q, grp):
        ref = wall.at[tap_of(grp), core, q]
        return pltpu.make_async_remote_copy(
            ref, ref, pair_send.at[grp], pair_recv.at[grp], device_id={"xy": mate}, device_id_type=MESH)

    def to_twin(h, grp):
        ref = wall.at[tap_of(grp), h]
        return pltpu.make_async_remote_copy(
            ref, ref, core_send.at[grp], core_recv.at[grp], device_id={"gz": twin}, device_id_type=MESH)

    def line_start(grp):
        for k in range(1, line):
            along(k, grp).start()

    def line_stage(grp):
        for k in range(1, line):
            from_line((pos + k) % line, grp).wait_recv()
        across(col, grp).start()

    def pair_stage(grp):
        across(1 - col, grp).wait_recv()
        to_twin(core, grp).start()

    def core_stage(grp):
        to_twin(1 - core, grp).wait_recv()

    def finish(grp):
        for k in range(1, line):
            along(k, grp).wait_send()
        across(col, grp).wait_send()
        to_twin(core, grp).wait_send()

    low = g < n // 2

    def tap_of(grp):
        return jnp.where(low | (grp < near_taps), grp, near_taps + taps - 1 - grp)

    def exchange(src, dst, send, recv, d):
        return pltpu.make_async_remote_copy(
            src.at[d], dst.at[g], send.at[d], recv.at[g], device_id={"gz": d}, device_id_type=MESH)

    def toward(d):
        return pltpu.make_async_remote_copy(
            ms.at[g], ms.at[g], m_send.at[d], m_recv.at[g], device_id={"gz": d}, device_id_type=MESH)

    def arrival(dst, send, recv, d):
        return pltpu.make_async_remote_copy(
            dst.at[d], dst.at[d], send.at[d], recv.at[d], device_id={"gz": d}, device_id_type=MESH)

    def split(value, ref, start, count):
        high = value.astype(jnp.bfloat16)
        low = (value - high.astype(jnp.float32)).astype(jnp.bfloat16)
        at = pl.ds(pl.multiple_of(start, 16), count)
        ref[at, 0:channels] = high
        ref[at, channels : 2 * channels] = low
        ref[at, 2 * channels :] = high

    def prepare(grp):
        core_stage(grp)
        tap = tap_of(grp)
        value = jnp.concatenate([wall[tap, h, q, p] for p in range(line) for q in range(2) for h in range(2)], axis=0)
        value = jnp.transpose(value)
        high = value.astype(jnp.bfloat16)
        low = (value - high.astype(jnp.float32)).astype(jnp.bfloat16)
        ready[grp, 0:channels] = high
        ready[grp, channels : 2 * channels] = high
        ready[grp, 2 * channels :] = low

    def product(lhs, weight):
        return jnp.dot(lhs, weight, preferred_element_type=jnp.float32)

    def columns(ref, picks):
        chosen = [ref[slab, pl.ds(row, 1), :] for slab, row in picks]
        chosen.append(jnp.zeros((-len(picks) % 8 + 8, 128), jnp.float32))
        r = lax.broadcasted_iota(jnp.int32, (plane, 128), 0)
        k = lax.broadcasted_iota(jnp.int32, (plane, 128), 1)
        block = (r % slab_x) // B * (span_y // B) + r // slab_x // B
        spots, chosen = (block == k).astype(jnp.float32), jnp.concatenate(chosen, axis=0)
        return lax.dot_general(spots, chosen, (((1,), (1,)), ((), ())), preferred_element_type=jnp.float32)

    def spread(flags, i):
        for z in range(deep):
            at = i * (deep // B) + z // B
            column = flags[:, at : at + 1]
            mf[i * rows + z * plane : i * rows + (z + 1) * plane, :] = jnp.broadcast_to(column, (plane, 128))

    def keep(at):
        return jnp.concatenate([mf[at]] * (channels // 128), axis=1)

    def mask_features(d):
        for z in range(deep):
            value = raw[d * deep + z].reshape(plane, channels)
            at = pl.ds(pl.multiple_of(d * rows + z * plane, 8), plane)
            stage[d, z * plane : (z + 1) * plane] = value * keep(at)

    def slab(i):
        return pl.ds(pl.multiple_of(i * rows, rows), rows)

    def near_tap(a, c):
        weight = ready[3 * a + c]
        base = pl.multiple_of((2 - a) * near_step * rows, rows)
        if c == 1:
            at = pl.ds(base, n * rows)
            acc[at] += product(xc[...], weight)
            return
        source, offset = (xl, skip) if c == 0 else (xh, 0)
        result = product(source[...], weight)
        for i in range(n * deep):
            at = pl.ds(pl.multiple_of(base + i * plane + offset, 8), edge)
            acc[at] += result[i * edge : (i + 1) * edge]

    def give(d):
        exchange(stage, xs, x_send, x_recv, d).wait_send()
        stage[d] = total[slab(d)] * keep(slab(d))
        exchange(stage, out, r_send, r_recv, d).start()

    def far_stage(order):
        weight = ready[near_taps + order]
        if order == 1:
            total[...] += product(hc[...], weight)
            return
        count = (n - far_step) * rows
        front = low if order == 0 else jnp.logical_not(low)
        source = pl.multiple_of(jnp.where(front, 0, far_step * rows), rows)
        target = pl.multiple_of(jnp.where(front, far_step * rows, 0), rows)
        total[pl.ds(target, count)] += product(hc[pl.ds(source, count)], weight)

    def turn(i, _):
        at = slab(i)
        value = jnp.maximum(acc[pl.ds(pl.multiple_of((i + near_step) * rows, rows), rows)], 0.0) * keep(at)
        split(value, hc, i * rows, rows)
        total[at] = xs[i]
        return 0

    def take_slab(i, _):
        value = xs[i]
        split(value, xc, i * rows, rows)
        planes = [value[z * plane : (z + 1) * plane] for z in range(deep)]
        split(jnp.concatenate([one[:edge] for one in planes], axis=0), xl, i * side, side)
        split(jnp.concatenate([one[skip:] for one in planes], axis=0), xh, i * side, side)
        return 0

    def step(tau):
        @pl.when(tau < taps)
        def _():
            line_stage(tau)

        @pl.when(tau + WINDOW < taps)
        def _():
            line_start(tau + WINDOW)

        @pl.when((tau >= LAG) & (tau < taps + LAG))
        def _():
            pair_stage(tau - LAG)

    def finish_all(grp, _):
        finish(grp)
        return 0

    def lead(tau, _):
        step(tau)

        @pl.when(tau >= 2 * LAG)
        def _():
            prepare(tau - 2 * LAG)

        return 0

    def near_row(a, _):
        for c in range(3):
            tap = 3 * a + c
            near_tap(a, c)
            step(tap + LEAD)

            @pl.when(tap + LEAD - 2 * LAG <= near_taps)
            def _():
                prepare(tap + LEAD - 2 * LAG)

        return 0

    for grp in range(WINDOW):
        line_start(grp)
    for load in loads[:2]:
        load.wait()
    ms[g] = jnp.zeros((ms.shape[1], 128), jnp.float32)
    for x in range(raw_mask.shape[1]):
        value = raw_mask[:, x, :].astype(jnp.float32)
        ms[g, :, x * (span_y // B) : (x + 1) * (span_y // B)] = value
    flags = columns(ms, [(g, j) for j in range(n * deep // B)])
    for i in range(n):
        spread(flags, i)
    for k in range(n):
        d = (g + n // 2 + k) % n
        mask_features(d)
        if k == n // 2:
            xs[g] = stage[g]
        else:
            exchange(stage, xs, x_send, x_recv, d).start()
            toward(d).start()

    lax.fori_loop(0, LEAD, lead, 0)
    acc[...] = jnp.zeros_like(acc)
    for i in range(1, n):
        d = (g + i) % n
        arrival(xs, x_send, x_recv, d).wait_recv()
        arrival(ms, m_send, m_recv, d).wait_recv()
    flags = columns(ms, [(i, g * (deep // B) + j) for i in range(n) for j in range(deep // B)])
    for i in range(n):
        spread(flags, i)
    lax.fori_loop(0, n, take_slab, 0)
    lax.fori_loop(0, 3, near_row, 0)
    lax.fori_loop(0, n, turn, 0)
    for order in range(3):
        far_stage(order)
        if order == 1:
            for i in range(n // 2):
                give(jnp.where(low, n // 2, 0) + i)
        if order < 2:
            prepare(near_taps + order + 1)
    for i in range(1, n // 2):
        give(g // (n // 2) * (n // 2) + (g + i) % (n // 2))

    stage[g] = total[slab(g)] * keep(slab(g))
    own = pltpu.make_async_copy(stage.at[g], out.at[g], out_sem)
    own.start()
    lax.fori_loop(0, taps, finish_all, 0)
    for i in range(1, n):
        d = (g + i) % n
        toward(d).wait_send()
        exchange(stage, out, r_send, r_recv, d).wait_send()
        arrival(out, r_send, r_recv, d).wait_recv()
    own.wait()


def fits(features, weight):
    slab_z, slab_x, span_y, channels = features.shape
    n, m = lax.axis_size("gz"), lax.axis_size("xy")
    deep, plane, part = slab_z // n, span_y * slab_x, weight.shape[2]
    return (
        FAR_DILATION >= span_y > NEAR_DILATION
        and NEAR_DILATION >= slab_x * m
        and NEAR_DILATION % slab_z == 0 and FAR_DILATION % slab_z == 0 and NEAR_DILATION < n * slab_z and FAR_DILATION < n * slab_z
        and n % 4 == 0 and 2 * FAR_DILATION >= n * slab_z and m % 2 == 0 and m >= 4
        and slab_z % (B * n) == 0 and slab_x % B == 0 and span_y % B == 0 and slab_z // B % 8 == 0
        and plane <= 128 and plane % 8 == 0 and NEAR_DILATION * slab_x % 8 == 0
        and deep * plane % 16 == 0 and deep * (span_y - NEAR_DILATION) * slab_x % 16 == 0
        and channels % 128 == 0 and part % 16 == 0 and part * m == channels
    )


def fast(features, block_mask, near_kernel_weight, far_kernel_weight):
    slab_z, slab_x, span_y, channels = features.shape
    n, m = lax.axis_size("gz"), lax.axis_size("xy")
    part = near_kernel_weight.shape[2]
    deep, plane = slab_z // n, span_y * slab_x
    rows, side = deep * plane, deep * (span_y - NEAR_DILATION) * slab_x
    near = jnp.swapaxes(near_kernel_weight, 1, 2)
    far = jnp.swapaxes(far_kernel_weight, 1, 2)
    feat = jnp.swapaxes(features, 1, 2)
    taps = 12
    line = m // 2
    dma = pltpu.SemaphoreType.DMA
    out = pl.pallas_call(
        functools.partial(section_kernel, n, deep, span_y, NEAR_DILATION // slab_z, FAR_DILATION // slab_z),
        out_shape=jax.ShapeDtypeStruct((n, rows, channels), jnp.float32),
        in_specs=[pl.BlockSpec(memory_space=pltpu.HBM)] * 4,
        out_specs=pl.BlockSpec(memory_space=pl.ANY),
        scratch_shapes=[
            pltpu.VMEM((taps, 2, 2, line, part // 2, channels), jnp.float32),
            pltpu.VMEM((taps, 3 * channels, m * part), jnp.bfloat16),
            pltpu.VMEM(feat.shape, jnp.float32),
            pltpu.VMEM(block_mask.shape, jnp.int32),
            pltpu.VMEM((n, rows, channels), jnp.float32),
            pltpu.VMEM((n, rows, channels), jnp.float32),
            pltpu.VMEM((n, slab_z // B, 128), jnp.float32),
            pltpu.VMEM((n * rows, 128), jnp.float32),
            pltpu.VMEM((n * rows, 3 * channels), jnp.bfloat16),
            pltpu.VMEM((n * side, 3 * channels), jnp.bfloat16),
            pltpu.VMEM((n * side, 3 * channels), jnp.bfloat16),
            pltpu.VMEM(((n + 2 * (NEAR_DILATION // slab_z)) * rows, channels), jnp.float32),
            pltpu.VMEM((n * rows, 3 * channels), jnp.bfloat16),
            pltpu.VMEM((n * rows, channels), jnp.float32),
            dma((line, taps)), dma((taps,)), dma((taps,)),
            dma((line, taps)), dma((taps,)), dma((taps,)),
            dma((n,)), dma((n,)), dma((n,)), dma((n,)), dma((n,)), dma((n,)), dma((8,)), dma,
        ],
        compiler_params=pltpu.CompilerParams(
            collective_id=0, has_side_effects=True, vmem_limit_bytes=60 * 1024 * 1024),
        cost_estimate=pl.CostEstimate(flops=3 * 10**9, bytes_accessed=4 * 10**6, transcendentals=0),
    )(feat, block_mask, near, far)
    return jnp.swapaxes(out.reshape(feat.shape), 1, 2)


def local(features, block_mask, near_kernel_weight, far_kernel_weight):
    form = fast if fits(features, near_kernel_weight) else general
    return form(features, block_mask, near_kernel_weight, far_kernel_weight)


def solution(mesh):
    in_specs = (
        P("gz", "xy", None, None),
        P("gz", "xy", None),
        P(None, None, "xy"),
        P(None, None, "xy"),
    )
    out_specs = P("gz", "xy", None, None)
    return jax.shard_map(local, mesh=mesh, in_specs=in_specs, out_specs=out_specs, check_vma=False)
```
